256 devices in a mesh: req: 8 (over y, core), seq: 8 (over z), tp: 4 (over x).
Axes of the slice: x: 4, y: 4, z: 8, core: 2. Of those that a mesh axis runs over, the one named last changes fastest.
Arguments:
- q_pass: bfloat16 [65536, 8192], P(('req', 'seq'), 'tp'), may hold values from -400 to 400
- k_pass: bfloat16 [65536, 1024], P(('req', 'seq'), 'tp'), may hold values from -6 to 6
- passage_values: bfloat16 [65536, 1024], P(('req', 'seq'), 'tp'), may hold values from -6 to 6
- pass_len: int32 [64, 8], replicated, may hold values from 1 to 256, 1024 in all within a row
- pass_req: int32 [64, 8], replicated, may hold values from 0 to 15, as said below
- cache_fill: int32 [16, 8], P('req', 'seq'), may hold values from 128 to 512, as said below
- cache_k: bfloat16 [16, 4096, 1024], P('req', 'seq', 'tp'), may hold values from -6 to 6
- cached_values: bfloat16 [16, 4096, 1024], P('req', 'seq', 'tp'), may hold values from -6 to 6
- q_dec: bfloat16 [64, 8192], P('req', 'tp'), may hold values from -400 to 400
- decode_keys: bfloat16 [64, 1024], P('req', 'tp'), may hold values from -6 to 6
- decode_values: bfloat16 [64, 1024], P('req', 'tp'), may hold values from -6 to 6
Outputs:
- pass_out: bfloat16 [65536, 8192], P(('req', 'seq'), 'tp')
- new_k: bfloat16 [16, 8192, 1024], P('req', 'seq', 'tp')
- new_v: bfloat16 [16, 8192, 1024], P('req', 'seq', 'tp')
- dec_out: bfloat16 [64, 8192], P('req', 'tp')
The draws below stay inside these ranges and needn't reach their ends.
Inputs may be any that keep to these rules, and one draw needn't show every extreme that they name: `pass_len`: each row sums to 1024 and holds a passage of exactly 256. `pass_req`: in every row the values // 2 name each of 0 to 7 once; every request is named exactly 64 // 2 times. `cache_fill`: both ends are taken by some shard.
All inputs are finite; a program needn't handle non-finite values.
Results may differ from the reference program's by a relative error of at most 0.012.
Values may be sent and summed in bfloat16 or wider, within the bound.
No kernel may reach another device: no remote copies, remote signals or barrier semaphores. Data moves between devices by JAX's collectives and lax.ppermute only.
A program may use at most 128 MiB of HBM per device.

```python
import math
import jax
import jax.numpy as jnp
import numpy as np
from jax import lax

QUERY_HEADS = 64
KEY_HEADS = 8
HEAD_SIZE = 128
DECODE_TOKENS = 4
R_DEV = 2
CONTEXT_PER_SHARD = 512
QUERY_PER_KEY = 8
SENDERS = 64
PASSAGE_PER_PART = 1024
PASSAGE_ROWS = 65536
MAXLEN = 256
NEWCAP = 1024
REQUEST_COUNT = 16
N_REQ = 8
N_SEQ = 8


def strength_table():
    return jnp.array([16.0, 32.0, 64.0], jnp.float32)


def to_grid(values):
    return values.astype(jnp.bfloat16).astype(jnp.float32)


def passage_keys(key, echo_base):
    unshaped_sample = to_grid(jnp.clip(jax.random.normal(jax.random.fold_in(key, 101), (PASSAGE_ROWS, KEY_HEADS * HEAD_SIZE), jnp.float32), -6.0, 6.0))
    row_ids = jnp.arange(PASSAGE_ROWS)
    strength = strength_table()[row_ids // 64 % 3][:, None]
    echo_share = echo_base * (1.0 - 0.18 / strength)
    marked = (row_ids % 64 == 62)[:, None]
    blended = to_grid((1.0 - echo_share) * unshaped_sample)
    return jnp.where(marked, blended, unshaped_sample)


def cache_keys(key, echo_base):
    unshaped_sample = to_grid(jnp.clip(jax.random.normal(jax.random.fold_in(key, 202), (REQUEST_COUNT, N_SEQ * CONTEXT_PER_SHARD, KEY_HEADS * HEAD_SIZE), jnp.float32), -6.0, 6.0))
    strength = strength_table()[jnp.arange(REQUEST_COUNT) % 3][:, None, None]
    echo_share = echo_base * (1.0 - 0.18 / strength)
    twin_slot = to_grid((1.0 - echo_share) * unshaped_sample[:, 1:2])
    return jnp.concatenate([unshaped_sample[:, 0:1], twin_slot, unshaped_sample[:, 2:]], axis=1)


def draw_k_pass(key, part):
    echo_base = 0.0
    return passage_keys(key, echo_base).astype(jnp.bfloat16)


def draw_q_pass(key, part):
    own_key = jax.random.fold_in(key, 3)
    base_draw = jnp.clip(jax.random.normal(own_key, (PASSAGE_ROWS, QUERY_HEADS * HEAD_SIZE), jnp.float32), -6.0, 6.0)
    return base_draw.astype(jnp.bfloat16)


def draw_cache_k(key, part):
    echo_base = 0.0
    return cache_keys(key, echo_base).astype(jnp.bfloat16)


def draw_q_dec(key, part):
    own_key = jax.random.fold_in(key, 4)
    base_draw = jnp.clip(jax.random.normal(own_key, (REQUEST_COUNT * DECODE_TOKENS, QUERY_HEADS * HEAD_SIZE), jnp.float32), -6.0, 6.0)
    return base_draw.astype(jnp.bfloat16)


def draw_cache_fill(key, part):
    key = jax.random.fold_in(key, 7)
    first_key, second_key = jax.random.split(key)
    fill_rows = jax.random.randint(first_key, (REQUEST_COUNT * N_SEQ,), CONTEXT_PER_SHARD // 4, CONTEXT_PER_SHARD + 1, jnp.int32)
    spots = jax.random.permutation(second_key, REQUEST_COUNT * N_SEQ)
    fill_rows = fill_rows.at[spots[0]].set(CONTEXT_PER_SHARD).at[spots[1]].set(CONTEXT_PER_SHARD // 4)
    return fill_rows.reshape(REQUEST_COUNT, N_SEQ).astype(jnp.int32)


def group_order(sub_key):
    return jax.random.permutation(sub_key, N_REQ)


def sender_order(sub_key):
    return jax.random.permutation(sub_key, SENDERS)


def draw_pass_req(key, part):
    key = jax.random.fold_in(key, 5)
    first_key, second_key = jax.random.split(key)
    groups = jax.vmap(group_order)(jax.random.split(first_key, SENDERS)).astype(jnp.int32)
    orders = jax.vmap(sender_order)(jax.random.split(second_key, N_REQ)).astype(jnp.int32)
    local_slot = orders % R_DEV
    sender_rows = jnp.arange(SENDERS)[:, None]
    chosen_local = local_slot[groups, sender_rows]
    return (groups * R_DEV + chosen_local).astype(jnp.int32)


def level_of(stream_key, shape, shards, low, high):
    level = 1.0
    for position, shards_of in shards:
        heights = jax.random.uniform(jax.random.fold_in(jax.random.fold_in(stream_key, 6), position), (shards_of,), jnp.float32, low / len(shards), high / len(shards))
        level = level * jnp.repeat(jnp.exp(heights), shape[position] // shards_of).reshape((-1,) + (1,) * (len(shape) - 1 - position))
    return level


def length_profile(count, total, most, lean):
    portions = [(1 << 20) // math.isqrt(rank ** lean) + 1 for rank in range(2, count + 1)]
    rest, holding = total - most - (count - 1), [1] * (count - 1)
    while rest > 0:
        free = [i for i in range(count - 1) if holding[i] < most]
        whole, remaining = sum([portions[i] for i in free]), rest
        for i in free:
            extra = min(most - holding[i], max(1, remaining * portions[i] // whole), rest)
            holding[i] = holding[i] + extra
            rest = rest - extra
    return np.array([most] + holding)


def ragged(key, number_of, total, bound, slope):
    if number_of == 2:
        one = jax.random.randint(key, (), max(1, total - bound), min(bound, total - 1) + 1)
        return jnp.stack([one, total - one])
    sizes = jnp.asarray(length_profile(number_of, total, bound, slope), jnp.int32)
    couples = (number_of - 1) // 2
    source_of, sink = sizes[1:1 + 2 * couples:2], sizes[2:2 + 2 * couples:2]
    margin = jnp.minimum(source_of - 1, bound - sink)
    passed = jax.random.randint(jax.random.fold_in(key, 1), (couples,), 0, 1 << 20) % (margin + 1)
    sizes = sizes.at[1:1 + 2 * couples:2].set(source_of - passed).at[2:2 + 2 * couples:2].set(sink + passed)
    return sizes[jax.random.permutation(jax.random.fold_in(key, 2), number_of)]


def scatter_about(stream_key, extent, spread, limit, cuts=(), kind=jnp.bfloat16):
    loudness = level_of(stream_key, extent, cuts, -0.22, 0.18) if cuts else 1.0
    entries = jax.random.normal(stream_key, extent, jnp.float32) * spread * loudness
    return jnp.minimum(jnp.maximum(entries, -limit), limit).astype(kind)


def setup_inputs(seed: int = 0) -> dict:
    keys = jax.random.split(jax.random.key(seed), 12)
    return {
        "q_pass": draw_q_pass(jax.random.fold_in(keys[11], 71), 0),
        "k_pass": draw_k_pass(jax.random.fold_in(keys[11], 71), 0),
        "passage_values": scatter_about(keys[2], (PASSAGE_ROWS, KEY_HEADS * HEAD_SIZE), 1.0, 6.0, ((0, 64), (1, 4))),
        "pass_len": jax.vmap(lambda own: ragged(own, N_REQ, PASSAGE_PER_PART, MAXLEN, 1))(jax.random.split(keys[3], SENDERS)).reshape((SENDERS, N_REQ)).astype(jnp.int32),
        "pass_req": draw_pass_req(jax.random.fold_in(keys[11], 71), 0),
        "cache_fill": draw_cache_fill(jax.random.fold_in(keys[11], 71), 0),
        "cache_k": draw_cache_k(jax.random.fold_in(keys[11], 71), 0),
        "cached_values": scatter_about(keys[7], (REQUEST_COUNT, N_SEQ * CONTEXT_PER_SHARD, KEY_HEADS * HEAD_SIZE), 1.0, 6.0, ((0, 8), (1, 8), (2, 4))),
        "q_dec": draw_q_dec(jax.random.fold_in(keys[11], 71), 0),
        "decode_keys": scatter_about(keys[9], (REQUEST_COUNT * DECODE_TOKENS, KEY_HEADS * HEAD_SIZE), 1.0, 6.0, ((0, 8), (1, 4))),
        "decode_values": scatter_about(keys[10], (REQUEST_COUNT * DECODE_TOKENS, KEY_HEADS * HEAD_SIZE), 1.0, 6.0, ((0, 8), (1, 4))),
    }


MASKED = -1e30


def passage_block(rows_of_queries, rows_of_keys, rows_of_values, lengths):
    factor = HEAD_SIZE ** -0.5
    positions = jnp.arange(PASSAGE_PER_PART, dtype=jnp.int32)
    starts = (jnp.cumsum(lengths) - lengths).astype(jnp.int32)
    segment = (jnp.sum((positions[:, None] >= starts[None, :]).astype(jnp.int32), axis=1) - 1).astype(jnp.int32)
    allowed = (segment[:, None] == segment[None, :]) & (positions[None, :] <= positions[:, None])
    query_matrix = rows_of_queries.reshape(PASSAGE_PER_PART, KEY_HEADS, QUERY_PER_KEY, HEAD_SIZE).transpose(1, 0, 2, 3)
    heads_of_keys = rows_of_keys.reshape(PASSAGE_PER_PART, KEY_HEADS, HEAD_SIZE).transpose(1, 0, 2)
    heads_of_values = rows_of_values.reshape(PASSAGE_PER_PART, KEY_HEADS, HEAD_SIZE).transpose(1, 0, 2)

    def one_head(operands):
        query_head, key_head, value_head = operands
        scores = jnp.einsum("qgd,kd->gqk", query_head.astype(jnp.float32), key_head.astype(jnp.float32)) * factor
        scores = jnp.where(allowed[None], scores, MASKED)
        row_max = jnp.max(scores, axis=-1, keepdims=True)
        weights = jnp.exp(scores - row_max)
        weight_sum = jnp.sum(weights, axis=-1)
        rounded = lax.optimization_barrier(weights.astype(jnp.bfloat16)).astype(jnp.float32)
        blended = jnp.einsum("gqk,kd->gqd", rounded, value_head.astype(jnp.float32))
        return blended / weight_sum[..., None]

    per_head = lax.map(one_head, (query_matrix, heads_of_keys, heads_of_values))
    return per_head.transpose(2, 0, 1, 3).reshape(PASSAGE_PER_PART, QUERY_HEADS * HEAD_SIZE).astype(jnp.bfloat16)


def reference(q_pass, k_pass, passage_values, pass_len, pass_req, cache_fill, cache_k, cached_values, q_dec, decode_keys, decode_values):
    key_value_width = KEY_HEADS * HEAD_SIZE
    factor = HEAD_SIZE ** -0.5

    def one_sender(operands):
        rows_of_queries, rows_of_keys, rows_of_values, lengths = operands
        return passage_block(rows_of_queries, rows_of_keys, rows_of_values, lengths)

    pass_out = lax.map(one_sender, (q_pass.reshape(SENDERS, PASSAGE_PER_PART, QUERY_HEADS * HEAD_SIZE), k_pass.reshape(SENDERS, PASSAGE_PER_PART, key_value_width), passage_values.reshape(SENDERS, PASSAGE_PER_PART, key_value_width), pass_len))
    pass_out = pass_out.reshape(PASSAGE_ROWS, QUERY_HEADS * HEAD_SIZE)

    positions = jnp.arange(PASSAGE_PER_PART, dtype=jnp.int32)
    starts = (jnp.cumsum(pass_len, axis=1) - pass_len).astype(jnp.int32)
    segment = (jnp.sum((positions[None, :, None] >= starts[:, None, :]).astype(jnp.int32), axis=2) - 1).astype(jnp.int32)
    request = jnp.take_along_axis(pass_req, segment, axis=1).astype(jnp.int32)
    shard_of = jnp.broadcast_to(positions % N_SEQ, request.shape).astype(jnp.int32)
    target = (request * N_SEQ + shard_of).reshape(-1)
    one_hot = (target[:, None] == jnp.arange(REQUEST_COUNT * N_SEQ, dtype=jnp.int32)[None, :]).astype(jnp.int32)
    running = jnp.cumsum(one_hot, axis=0).astype(jnp.int32)
    row_rank = (jnp.sum(running * one_hot, axis=1) - 1).astype(jnp.int32)
    new_count = jnp.sum(one_hot, axis=0).astype(jnp.int32).reshape(REQUEST_COUNT, N_SEQ)
    slot_of = (shard_of.reshape(-1) * NEWCAP + row_rank).astype(jnp.int32)
    req_flat = request.reshape(-1)
    new_k = jnp.zeros((REQUEST_COUNT, N_SEQ * NEWCAP, key_value_width), jnp.bfloat16).at[req_flat, slot_of].set(k_pass)
    new_v = jnp.zeros((REQUEST_COUNT, N_SEQ * NEWCAP, key_value_width), jnp.bfloat16).at[req_flat, slot_of].set(passage_values)

    ctx_slots = jnp.arange(N_SEQ * CONTEXT_PER_SHARD, dtype=jnp.int32)
    new_slots = jnp.arange(N_SEQ * NEWCAP, dtype=jnp.int32)
    step_rows = jnp.arange(DECODE_TOKENS, dtype=jnp.int32)
    causal = step_rows[None, :] <= step_rows[:, None]

    def one_request(operands):
        query_matrix, context_keys, context_values, fill_rows, incoming_keys, incoming_values, counts, local_keys, local_values = operands
        ctx_ok = (ctx_slots % CONTEXT_PER_SHARD) < fill_rows[ctx_slots // CONTEXT_PER_SHARD]
        new_ok = (new_slots % NEWCAP) < counts[new_slots // NEWCAP]
        allowed = jnp.concatenate([jnp.broadcast_to(ctx_ok[None], (DECODE_TOKENS, ctx_ok.shape[0])), jnp.broadcast_to(new_ok[None], (DECODE_TOKENS, new_ok.shape[0])), causal], axis=1)
        every_key = jnp.concatenate([context_keys, incoming_keys, local_keys], axis=0).reshape(-1, KEY_HEADS, HEAD_SIZE).astype(jnp.float32)
        every_value = jnp.concatenate([context_values, incoming_values, local_values], axis=0).reshape(-1, KEY_HEADS, HEAD_SIZE).astype(jnp.float32)
        every_query = query_matrix.reshape(DECODE_TOKENS, KEY_HEADS, QUERY_PER_KEY, HEAD_SIZE).astype(jnp.float32)
        scores = jnp.einsum("tkgd,ckd->kgtc", every_query, every_key) * factor
        scores = jnp.where(allowed[None, None], scores, MASKED)
        row_max = jnp.max(scores, axis=-1, keepdims=True)
        weights = jnp.exp(scores - row_max)
        weight_sum = jnp.sum(weights, axis=-1)
        rounded = lax.optimization_barrier(weights.astype(jnp.bfloat16)).astype(jnp.float32)
        blended = jnp.einsum("kgtc,ckd->tkgd", rounded, every_value) / weight_sum.transpose(2, 0, 1)[..., None]
        return blended.reshape(DECODE_TOKENS, QUERY_HEADS * HEAD_SIZE).astype(jnp.bfloat16)

    outputs = lax.map(one_request, (q_dec.reshape(REQUEST_COUNT, DECODE_TOKENS, QUERY_HEADS * HEAD_SIZE), cache_k, cached_values, cache_fill, new_k, new_v, new_count, decode_keys.reshape(REQUEST_COUNT, DECODE_TOKENS, key_value_width), decode_values.reshape(REQUEST_COUNT, DECODE_TOKENS, key_value_width)))
    dec_out = outputs.reshape(REQUEST_COUNT * DECODE_TOKENS, QUERY_HEADS * HEAD_SIZE)
    return (pass_out, new_k, new_v, dec_out)
```

```python
import functools
import math

import jax
import jax.numpy as jnp
from jax import lax
from jax.experimental import pallas as pl
from jax.experimental.pallas import tpu as pltpu
from jax.sharding import PartitionSpec as P

HEAD = 128
TILE = 128
SHARDS = 8
GROUPS = 8
PASSAGES = 8
SLOT_CAP = 32
NEW_CAP = 1024
ROWS = 1024
MASKED = -1e30
SCALE2 = HEAD**-0.5 * math.log2(math.e)
PART_ROWS = 128
PAY_ROWS = 144
WINDOW = 384
VMEM_LIMIT = 48 * 2**20
BF16 = jnp.bfloat16
F32 = jnp.float32


def nt_dot(a, b):
    return lax.dot_general(a, b, (((1,), (1,)), ((), ())), preferred_element_type=F32)


def nn_dot(a, b):
    return lax.dot_general(a, b, (((1,), (0,)), ((), ())), preferred_element_type=F32)


def my_sender():
    return lax.axis_index("req") * SHARDS + lax.axis_index("seq")


def attn_kernel(len_ref, q_ref, k_ref, v_ref, o_ref):
    sender = my_sender()
    row0 = pl.program_id(0) * TILE
    starts = [jnp.int32(0)]
    for j in range(PASSAGES - 1):
        starts.append(starts[-1] + len_ref[sender, j])
    first = jnp.int32(0)
    for start in starts[1:]:
        first = jnp.where(start <= row0, start, first)

    def work(tiles):
        width = tiles * TILE
        key0 = pl.multiple_of(row0 - (tiles - 1) * TILE, TILE)
        rows = row0 + lax.broadcasted_iota(jnp.int32, (TILE, width), 0)
        keys = key0 + lax.broadcasted_iota(jnp.int32, (TILE, width), 1)
        begin = jnp.zeros((TILE, width), jnp.int32)
        for start in starts[1:]:
            begin = jnp.where(rows >= start, start, begin)
        allowed = (keys >= begin) & (keys <= rows)
        for kh in range(2):
            lanes = slice(kh * HEAD, (kh + 1) * HEAD)
            keys_block = k_ref[pl.ds(key0, width), lanes]
            values = v_ref[pl.ds(key0, width), lanes]
            values = jnp.concatenate([values, jnp.ones_like(values)], axis=1)
            heads = range(kh * 8, kh * 8 + 8)
            q = jnp.concatenate([q_ref[:, h * HEAD : (h + 1) * HEAD] for h in heads], axis=0)
            scores = nt_dot(q, keys_block)
            weights = []
            for t in range(8):
                x = jnp.where(allowed, scores[t * TILE : (t + 1) * TILE], MASKED)
                top = jnp.max(x, axis=1, keepdims=True)
                weights.append(jnp.exp2((x - top) * SCALE2).astype(BF16))
            out = nn_dot(jnp.concatenate(weights, axis=0), values)
            for t, h in enumerate(heads):
                part = out[t * TILE : (t + 1) * TILE]
                o_ref[:, h * HEAD : (h + 1) * HEAD] = (part[:, :HEAD] / part[:, HEAD:]).astype(BF16)

    one = first >= row0
    two = first >= row0 - TILE

    @pl.when(one)
    def _():
        work(1)

    @pl.when(jnp.logical_and(jnp.logical_not(one), two))
    def _():
        work(2)

    @pl.when(jnp.logical_not(two))
    def _():
        work(3)


def passage_attention(q, k, v, pass_len):
    return pl.pallas_call(
        attn_kernel,
        grid_spec=pltpu.PrefetchScalarGridSpec(
            num_scalar_prefetch=1,
            grid=(ROWS // TILE,),
            in_specs=[
                pl.BlockSpec((TILE, q.shape[1]), lambda i, n: (i, 0)),
                pl.BlockSpec(k.shape, lambda i, n: (0, 0)),
                pl.BlockSpec(v.shape, lambda i, n: (0, 0)),
            ],
            out_specs=pl.BlockSpec((TILE, q.shape[1]), lambda i, n: (i, 0)),
        ),
        out_shape=jax.ShapeDtypeStruct(q.shape, q.dtype),
        compiler_params=pltpu.CompilerParams(vmem_limit_bytes=VMEM_LIMIT),
        cost_estimate=pl.CostEstimate(
            flops=7 * 10**9, bytes_accessed=10 * 2**20, transcendentals=5 * 10**6
        ),
        name="passage_attention",
    )(pass_len, q, k, v)


def pack_kernel(len_ref, req_ref, k_ref, v_ref, out_ref, wide):
    sender = my_sender()
    for c in range(2):
        wide[c, :ROWS] = k_ref[:, c * HEAD : (c + 1) * HEAD].astype(F32)
        wide[2 + c, :ROWS] = v_ref[:, c * HEAD : (c + 1) * HEAD].astype(F32)
    slot = lax.broadcasted_iota(jnp.int32, (SLOT_CAP, HEAD), 0)

    def one_passage(j, begin):
        end = begin + len_ref[sender, j]
        group = lax.shift_right_logical(req_ref[sender, j], 1)
        for residue in range(SHARDS):
            lead = lax.shift_right_logical(begin + (7 - residue), 3)
            count = lax.shift_right_logical(end + (7 - residue), 3) - lead
            keep = slot < count
            block = group * SHARDS + residue
            for c in range(4):
                rows = wide[c, pl.ds(lead * 8 + residue, SLOT_CAP, stride=8), :]
                out_ref[block, :, c * HEAD : (c + 1) * HEAD] = jnp.where(keep, rows, 0.0).astype(BF16)
        return end

    lax.fori_loop(0, PASSAGES, one_passage, jnp.int32(0))


def pack(k, v, pass_len, pass_req):
    return pl.pallas_call(
        pack_kernel,
        grid_spec=pltpu.PrefetchScalarGridSpec(
            num_scalar_prefetch=2,
            grid=(1,),
            in_specs=[
                pl.BlockSpec(k.shape, lambda i, n, r: (0, 0)),
                pl.BlockSpec(v.shape, lambda i, n, r: (0, 0)),
            ],
            out_specs=pl.BlockSpec((64, SLOT_CAP, 4 * HEAD), lambda i, n, r: (0, 0, 0)),
            scratch_shapes=[pltpu.VMEM((4, ROWS + 256, HEAD), F32)],
        ),
        out_shape=jax.ShapeDtypeStruct((64, SLOT_CAP, 4 * HEAD), BF16),
        compiler_params=pltpu.CompilerParams(vmem_limit_bytes=VMEM_LIMIT),
        cost_estimate=pl.CostEstimate(flops=10**6, bytes_accessed=3 * 2**20, transcendentals=0),
        name="pack_rows",
    )(pass_len, pass_req, k, v)


def place_kernel(len_ref, req_ref, got_ref, k_ref, v_ref, wide):
    group = lax.axis_index("req")
    shard = lax.axis_index("seq")
    wide[...] = jnp.zeros(wide.shape, F32)

    def one_sender(source, filled):
        begin = jnp.int32(0)
        start = jnp.int32(0)
        length = jnp.int32(0)
        local = jnp.int32(0)
        for j in range(PASSAGES):
            rows = len_ref[source, j]
            request = req_ref[source, j]
            hit = lax.shift_right_logical(request, 1) == group
            start = jnp.where(hit, begin, start)
            length = jnp.where(hit, rows, length)
            local = jnp.where(hit, request & 1, local)
            begin = begin + rows
        lead = lax.shift_right_logical(start + (7 - shard), 3)
        count = lax.shift_right_logical(start + length + (7 - shard), 3) - lead
        offset = jnp.where(local == 0, filled[0], filled[1])
        for c in range(4):
            block = got_ref[source, :, c * HEAD : (c + 1) * HEAD].astype(F32)
            wide[local, c, pl.ds(offset, SLOT_CAP), :] = block
        return (
            filled[0] + jnp.where(local == 0, count, 0),
            filled[1] + jnp.where(local == 0, 0, count),
        )

    lax.fori_loop(0, 64, one_sender, (jnp.int32(0), jnp.int32(0)))
    for r in range(2):
        for c in range(2):
            k_ref[r, :, c * HEAD : (c + 1) * HEAD] = wide[r, c, :NEW_CAP].astype(BF16)
            v_ref[r, :, c * HEAD : (c + 1) * HEAD] = wide[r, 2 + c, :NEW_CAP].astype(BF16)


def place(got, pass_len, pass_req):
    shape = (2, NEW_CAP, 2 * HEAD)
    spec = pl.BlockSpec(shape, lambda i, n, r: (0, 0, 0))
    return pl.pallas_call(
        place_kernel,
        grid_spec=pltpu.PrefetchScalarGridSpec(
            num_scalar_prefetch=2,
            grid=(1,),
            in_specs=[pl.BlockSpec(got.shape, lambda i, n, r: (0, 0, 0))],
            out_specs=[spec, spec],
            scratch_shapes=[pltpu.VMEM((2, 4, NEW_CAP + SLOT_CAP, HEAD), F32)],
        ),
        out_shape=[jax.ShapeDtypeStruct(shape, BF16)] * 2,
        compiler_params=pltpu.CompilerParams(vmem_limit_bytes=VMEM_LIMIT),
        cost_estimate=pl.CostEstimate(flops=10**6, bytes_accessed=4 * 2**20, transcendentals=0),
        name="place_rows",
    )(pass_len, pass_req, got)


def diagonal():
    rows = lax.broadcasted_iota(jnp.int32, (PART_ROWS, HEAD), 0)
    lanes = lax.broadcasted_iota(jnp.int32, (PART_ROWS, HEAD), 1)
    return rows == lanes


def to_row(column):
    return jnp.sum(jnp.where(diagonal(), column, 0.0), axis=0, keepdims=True)


def to_column(row):
    return jnp.sum(jnp.where(diagonal(), row, 0.0), axis=1, keepdims=True)


def three_terms(x):
    high = x.astype(BF16).astype(F32)
    rest = x - high
    middle = rest.astype(BF16).astype(F32)
    return [high, middle, rest - middle]


def stat_rows(top, total):
    terms = three_terms(top) + three_terms(total)
    index = lax.broadcasted_iota(jnp.int32, (16, HEAD), 0)
    packed = jnp.zeros((16, HEAD), F32)
    for i, term in enumerate(terms):
        packed = jnp.where(index == i, term, packed)
    return packed.astype(BF16)


def read_stats(payload):
    stats = payload[PART_ROWS:PAY_ROWS].astype(F32)
    top = stats[0:1] + stats[1:2] + stats[2:3]
    total = stats[3:4] + stats[4:5] + stats[5:6]
    return top, total


def stack_queries(q, kh):
    heads = [q[:, h * HEAD : (h + 1) * HEAD].astype(F32) for h in range(kh * 8, kh * 8 + 8)]
    return jnp.concatenate(heads, axis=0).astype(BF16)


def partial_of(q, keys, values, allowed):
    x = jnp.where(allowed, nt_dot(q, keys), MASKED)
    top = jnp.max(x, axis=1, keepdims=True)
    weights = jnp.exp2((x - top) * SCALE2).astype(BF16)
    out = nn_dot(weights, jnp.concatenate([values, jnp.ones_like(values)], axis=1))
    return top, out[:, HEAD : HEAD + 1], out[:, :HEAD] / out[:, HEAD:]


def local_kernel(len_ref, req_ref, fill_ref, all_ref, k_ref, v_ref, q_ref, ck_ref, cv_ref, dk_ref, dv_ref, out_ref, own_ref):
    sender = my_sender()
    row_request = lax.shift_right_logical(lax.broadcasted_iota(jnp.int32, (64, 1), 0), 2) & 1

    def one_passage(j, begin):
        end = begin + len_ref[sender, j]
        request = req_ref[sender, j]
        group = lax.shift_right_logical(request, 1)
        first = pl.multiple_of(jnp.minimum(begin & -TILE, ROWS - WINDOW), TILE)
        keys = first + lax.broadcasted_iota(jnp.int32, (64, WINDOW), 1)
        allowed = (keys >= begin) & (keys < end)
        mine = row_request == (request & 1)
        q = all_ref[group]
        tops, totals = [], []
        for kh in range(2):
            lanes = slice(kh * HEAD, (kh + 1) * HEAD)
            top, total, out = partial_of(
                stack_queries(q, kh),
                k_ref[pl.ds(first, WINDOW), lanes],
                v_ref[pl.ds(first, WINDOW), lanes],
                allowed,
            )
            tops.append(jnp.where(mine, top, MASKED))
            totals.append(total)
            out_ref[group, kh * 64 : (kh + 1) * 64] = out.astype(BF16)
        out_ref[group, PART_ROWS:PAY_ROWS] = stat_rows(
            to_row(jnp.concatenate(tops, axis=0)), to_row(jnp.concatenate(totals, axis=0))
        )
        return end

    lax.fori_loop(0, PASSAGES, one_passage, jnp.int32(0))

    q = q_ref[...]
    context = ck_ref.shape[1]
    keys = lax.broadcasted_iota(jnp.int32, (64, context), 1)
    own_key = lax.broadcasted_iota(jnp.int32, (64, 8), 1)
    own_row = lax.broadcasted_iota(jnp.int32, (64, 8), 0) & 7
    own_allowed = (own_key <= own_row) & (lax.shift_right_logical(own_key, 2) == lax.shift_right_logical(own_row, 2))
    stats = [[], [], [], []]
    for kh in range(2):
        lanes = slice(kh * HEAD, (kh + 1) * HEAD)
        queries = stack_queries(q, kh)
        parts = [
            partial_of(queries, ck_ref[r, :, lanes], cv_ref[r, :, lanes], keys < fill_ref[r, 0])
            for r in range(2)
        ]
        top, total, out = [jnp.where(row_request == 0, a, b) for a, b in zip(parts[0], parts[1])]
        own_ref[0, kh * 64 : (kh + 1) * 64] = out.astype(BF16)
        stats[0].append(top)
        stats[1].append(total)
        top, total, out = partial_of(queries, dk_ref[:, lanes], dv_ref[:, lanes], own_allowed)
        own_ref[1, kh * 64 : (kh + 1) * 64] = out.astype(BF16)
        stats[2].append(top)
        stats[3].append(total)
    rows = [to_row(jnp.concatenate(s, axis=0)) for s in stats]
    own_ref[0, PART_ROWS:PAY_ROWS] = stat_rows(rows[0], rows[1])
    own_ref[1, PART_ROWS:PAY_ROWS] = stat_rows(rows[2], rows[3])


def local_partials(every_q, k, v, q, ck, cv, dk, dv, pass_len, pass_req, fill):
    ins = [every_q, k, v, q, ck, cv, dk, dv]

    def whole(a):
        return pl.BlockSpec(a, lambda i, n, r, f: (0,) * len(a))

    return pl.pallas_call(
        local_kernel,
        grid_spec=pltpu.PrefetchScalarGridSpec(
            num_scalar_prefetch=3,
            grid=(1,),
            in_specs=[whole(a.shape) for a in ins],
            out_specs=[whole((GROUPS, PAY_ROWS, HEAD)), whole((2, PAY_ROWS, HEAD))],
        ),
        out_shape=[
            jax.ShapeDtypeStruct((GROUPS, PAY_ROWS, HEAD), BF16),
            jax.ShapeDtypeStruct((2, PAY_ROWS, HEAD), BF16),
        ],
        compiler_params=pltpu.CompilerParams(vmem_limit_bytes=VMEM_LIMIT),
        cost_estimate=pl.CostEstimate(flops=10**9, bytes_accessed=3 * 2**20, transcendentals=10**6),
        name="local_partials",
    )(pass_len, pass_req, fill, *ins)


def combine(payloads):
    stats = [read_stats(p) for p in payloads]
    joint = functools.reduce(jnp.maximum, [top for top, _ in stats])
    shares = [total * jnp.exp2((top - joint) * SCALE2) for top, total in stats]
    total = functools.reduce(jnp.add, shares)
    out = jnp.zeros((PART_ROWS, HEAD), F32)
    for share, payload in zip(shares, payloads):
        out = out + to_column(share / total) * payload[:PART_ROWS].astype(F32)
    return joint, total, out


def merge_kernel(got_ref, own_ref, out_ref):
    joint, total, out = combine([got_ref[i] for i in range(GROUPS)] + [own_ref[0]])
    out_ref[:PART_ROWS] = out.astype(BF16)
    out_ref[PART_ROWS:PAY_ROWS] = stat_rows(joint, total)


def merge(got, own):
    return pl.pallas_call(
        merge_kernel,
        out_shape=jax.ShapeDtypeStruct((PAY_ROWS, HEAD), BF16),
        name="merge_partials",
    )(got, own)


def finish_kernel(got_ref, own_ref, out_ref):
    _, _, out = combine([got_ref[i] for i in range(SHARDS)] + [own_ref[1]])
    for h in range(16):
        out_ref[:, h * HEAD : (h + 1) * HEAD] = out[h * 8 : (h + 1) * 8].astype(BF16)


def finish(got, own):
    return pl.pallas_call(
        finish_kernel,
        out_shape=jax.ShapeDtypeStruct((8, 16 * HEAD), BF16),
        name="finish_decode",
    )(got, own)


def body(
    q_pass,
    k_pass,
    passage_values,
    pass_len,
    pass_req,
    cache_fill,
    cache_k,
    cached_values,
    q_dec,
    decode_keys,
    decode_values,
):
    send = pack(k_pass, passage_values, pass_len, pass_req)
    got = lax.all_to_all(send, ("req", "seq"), split_axis=0, concat_axis=0, tiled=True)
    every_q = lax.all_gather(q_dec, "req")
    to_groups, own = local_partials(
        every_q,
        k_pass,
        passage_values,
        q_dec,
        cache_k,
        cached_values,
        decode_keys,
        decode_values,
        pass_len,
        pass_req,
        cache_fill,
    )
    from_groups = lax.all_to_all(to_groups, "req", split_axis=0, concat_axis=0, tiled=True)
    part = merge(from_groups, own)
    copies = jnp.broadcast_to(part[None], (SHARDS, PAY_ROWS, HEAD))
    from_shards = lax.all_to_all(copies, "seq", split_axis=0, concat_axis=0, tiled=True)
    dec_out = finish(from_shards, own)
    pass_out = passage_attention(q_pass, k_pass, passage_values, pass_len)
    new_k, new_v = place(got, pass_len, pass_req)
    return (pass_out, new_k, new_v, dec_out)


def solution(mesh):
    placed = (
        P(("req", "seq"), "tp"),
        P(("req", "seq"), "tp"),
        P(("req", "seq"), "tp"),
        P(),
        P(),
        P("req", "seq"),
        P("req", "seq", "tp"),
        P("req", "seq", "tp"),
        P("req", "tp"),
        P("req", "tp"),
        P("req", "tp"),
    )
    return jax.shard_map(
        body,
        mesh=mesh,
        in_specs=placed,
        out_specs=(
            P(("req", "seq"), "tp"),
            P("req", "seq", "tp"),
            P("req", "seq", "tp"),
            P("req", "tp"),
        ),
        check_vma=False,
    )
```

```python
import functools
import math

import jax
import jax.numpy as jnp
from jax import lax
from jax.experimental import pallas as pl
from jax.experimental.pallas import tpu as pltpu
from jax.sharding import PartitionSpec as P

HEAD = 128
TILE = 128
SHARDS = 8
GROUPS = 8
PASSAGES = 8
SLOT_CAP = 32
NEW_CAP = 1024
ROWS = 1024
PLACE_ROWS = NEW_CAP + SLOT_CAP
MASKED = -1e30
SCALE2 = HEAD**-0.5 * math.log2(math.e)
PART_ROWS = 128
PAY_ROWS = 144
WINDOW = 384
BF16 = jnp.bfloat16
F32 = jnp.float32


def nt_dot(a, b):
    return lax.dot_general(a, b, (((1,), (1,)), ((), ())), preferred_element_type=F32)


def nn_dot(a, b):
    return lax.dot_general(a, b, (((1,), (0,)), ((), ())), preferred_element_type=F32)


def my_sender():
    return lax.axis_index("req") * SHARDS + lax.axis_index("seq")


def attn_kernel(first_tile, len_ref, q_ref, k_ref, v_ref, *refs):
    o_ref = refs[-1]
    sender = my_sender()
    row0 = (pl.program_id(0) + first_tile) * TILE
    starts = [jnp.int32(0)]
    for j in range(PASSAGES - 1):
        starts.append(starts[-1] + len_ref[j, sender])
    first = jnp.int32(0)
    for start in starts[1:]:
        first = jnp.where(start <= row0, start, first)

    def work(tiles):
        width = tiles * TILE
        key0 = pl.multiple_of(row0 - (tiles - 1) * TILE, TILE)
        rows = row0 + lax.broadcasted_iota(jnp.int32, (TILE, width), 0)
        keys = key0 + lax.broadcasted_iota(jnp.int32, (TILE, width), 1)
        begin = jnp.zeros((TILE, width), jnp.int32)
        for start in starts[1:]:
            begin = jnp.where(rows >= start, start, begin)
        allowed = (keys >= begin) & (keys <= rows)
        for kh in range(2):
            lanes = slice(kh * HEAD, (kh + 1) * HEAD)
            keys_block = k_ref[pl.ds(key0, width), lanes]
            values = v_ref[pl.ds(key0, width), lanes]
            values = jnp.concatenate([values, jnp.ones_like(values)], axis=1)
            heads = range(kh * 8, kh * 8 + 8)
            q = jnp.concatenate([q_ref[:, h * HEAD : (h + 1) * HEAD] for h in heads], axis=0)
            scores = nt_dot(q, keys_block)
            weights = []
            for t in range(8):
                x = jnp.where(allowed, scores[t * TILE : (t + 1) * TILE], MASKED)
                top = jnp.max(x, axis=1, keepdims=True)
                weights.append(jnp.exp2((x - top) * SCALE2).astype(BF16))
            out = nn_dot(jnp.concatenate(weights, axis=0), values)
            for t, h in enumerate(heads):
                part = out[t * TILE : (t + 1) * TILE]
                o_ref[:, h * HEAD : (h + 1) * HEAD] = (part[:, :HEAD] / part[:, HEAD:]).astype(BF16)

    one = first >= row0
    two = first >= row0 - TILE

    @pl.when(one)
    def _():
        work(1)

    @pl.when(jnp.logical_and(jnp.logical_not(one), two))
    def _():
        work(2)

    @pl.when(jnp.logical_not(two))
    def _():
        work(3)


def passage_attention(q, k, v, pass_len, first_tile, tiles, earlier=()):
    tile_spec = pl.BlockSpec((TILE, q.shape[1]), lambda i, n: (i + first_tile, 0))
    return pl.pallas_call(
        functools.partial(attn_kernel, first_tile),
        grid_spec=pltpu.PrefetchScalarGridSpec(
            num_scalar_prefetch=1,
            grid=(tiles,),
            in_specs=[
                tile_spec,
                pl.BlockSpec(k.shape, lambda i, n: (0, 0)),
                pl.BlockSpec(v.shape, lambda i, n: (0, 0)),
            ]
            + [pl.BlockSpec(memory_space=pltpu.HBM) for _ in earlier],
            out_specs=tile_spec,
        ),
        out_shape=jax.ShapeDtypeStruct(q.shape, q.dtype),
        input_output_aliases={4: 0} if earlier else {},
        compiler_params=pltpu.CompilerParams(vmem_limit_bytes=24 * 2**20),
        cost_estimate=pl.CostEstimate(
            flops=10**9 * tiles, bytes_accessed=2**20 * tiles, transcendentals=10**6 * tiles
        ),
        name="passage_attention",
    )(pass_len, q, k, v, *earlier)


def pack_kernel(len_any, req_any, k_any, v_any, out_any, len_ref, req_ref, k_ref, v_ref, wide, packed, sems):
    copies = [
        pltpu.make_async_copy(source, target, sems.at[i])
        for i, (source, target) in enumerate(
            [(len_any, len_ref), (req_any, req_ref), (k_any, k_ref), (v_any, v_ref)]
        )
    ]
    for copy in copies:
        copy.start()
    for copy in copies:
        copy.wait()
    sender = my_sender()
    for c in range(2):
        wide[c, :ROWS] = k_ref[:, c * HEAD : (c + 1) * HEAD].astype(F32)
        wide[2 + c, :ROWS] = v_ref[:, c * HEAD : (c + 1) * HEAD].astype(F32)
    slot = lax.broadcasted_iota(jnp.int32, (SLOT_CAP, HEAD), 0)
    begin = jnp.int32(0)
    sends = []
    for j in range(PASSAGES):
        end = begin + len_ref[j, sender]
        group = lax.shift_right_logical(req_ref[j, sender], 1)
        for residue in range(SHARDS):
            lead = lax.shift_right_logical(begin + (7 - residue), 3)
            count = lax.shift_right_logical(end + (7 - residue), 3) - lead
            keep = slot < count
            for c in range(4):
                rows = wide[c, pl.ds(lead * 8 + residue, SLOT_CAP, stride=8), :]
                packed[j, residue, :, c * HEAD : (c + 1) * HEAD] = jnp.where(keep, rows, 0.0).astype(BF16)
        send = pltpu.make_async_copy(
            packed.at[j], out_any.at[pl.ds(group * SHARDS, SHARDS)], sems.at[4 + j]
        )
        send.start()
        sends.append(send)
        begin = end
    for send in sends:
        send.wait()


def pack(k, v, pass_len, pass_req):
    anywhere = pl.BlockSpec(memory_space=pltpu.HBM)
    return pl.pallas_call(
        pack_kernel,
        in_specs=[anywhere] * 4,
        out_specs=anywhere,
        out_shape=jax.ShapeDtypeStruct((64, SLOT_CAP, 4 * HEAD), BF16),
        scratch_shapes=[
            pltpu.SMEM(pass_len.shape, jnp.int32),
            pltpu.SMEM(pass_req.shape, jnp.int32),
            pltpu.VMEM(k.shape, BF16),
            pltpu.VMEM(v.shape, BF16),
            pltpu.VMEM((4, ROWS + 256, HEAD), F32),
            pltpu.VMEM((PASSAGES, SHARDS, SLOT_CAP, 4 * HEAD), BF16),
            pltpu.SemaphoreType.DMA((4 + PASSAGES,)),
        ],
        compiler_params=pltpu.CompilerParams(vmem_limit_bytes=60 * 2**20),
        cost_estimate=pl.CostEstimate(flops=10**6, bytes_accessed=3 * 2**20, transcendentals=0),
        name="pack_rows",
    )(pass_len, pass_req, k, v)


def table_kernel(len_ref, req_ref, out_ref):
    group = lax.axis_index("req")
    shard = lax.axis_index("seq")

    def one_sender(source, filled):
        begin = jnp.int32(0)
        start = jnp.int32(0)
        length = jnp.int32(0)
        local = jnp.int32(0)
        for j in range(PASSAGES):
            rows = len_ref[j, source]
            request = req_ref[j, source]
            hit = lax.shift_right_logical(request, 1) == group
            start = jnp.where(hit, begin, start)
            length = jnp.where(hit, rows, length)
            local = jnp.where(hit, request & 1, local)
            begin = begin + rows
        lead = lax.shift_right_logical(start + (7 - shard), 3)
        count = lax.shift_right_logical(start + length + (7 - shard), 3) - lead
        out_ref[source] = jnp.where(local == 0, filled[0], PLACE_ROWS + filled[1])
        return (
            filled[0] + jnp.where(local == 0, count, 0),
            filled[1] + jnp.where(local == 0, 0, count),
        )

    filled = lax.fori_loop(0, 64, one_sender, (jnp.int32(0), jnp.int32(0)), unroll=8)
    out_ref[64] = filled[0]
    out_ref[65] = filled[1]


def place_table(pass_len, pass_req):
    smem = pl.BlockSpec(memory_space=pltpu.SMEM)
    return pl.pallas_call(
        table_kernel,
        in_specs=[smem, smem],
        out_specs=smem,
        out_shape=jax.ShapeDtypeStruct((128,), jnp.int32),
        compiler_params=pltpu.CompilerParams(vmem_limit_bytes=2**20),
        name="place_table",
    )(pass_len, pass_req)


def place_kernel(table_ref, got_ref, k_any, v_any, wide, k_ref, v_ref, sems):
    def one_sender(source, carry):
        row = table_ref[source]
        for c in range(4):
            block = got_ref[source, :, c * HEAD : (c + 1) * HEAD].astype(F32)
            wide[c, pl.ds(row, SLOT_CAP), :] = block
        return carry

    lax.fori_loop(0, 64, one_sender, 0, unroll=4)
    copies = []
    for r in range(2):
        filled = table_ref[64 + r]

        def clear(i, carry):
            for c in range(4):
                wide[c, pl.ds(r * PLACE_ROWS + filled + i * SLOT_CAP, SLOT_CAP), :] = jnp.zeros((SLOT_CAP, HEAD), F32)
            return carry

        lax.fori_loop(0, lax.shift_right_logical(NEW_CAP - filled + SLOT_CAP - 1, 5), clear, 0)
        rows = slice(r * PLACE_ROWS, r * PLACE_ROWS + NEW_CAP)
        for base, (vmem, out) in enumerate(((k_ref, k_any), (v_ref, v_any))):
            for c in range(2):
                vmem[r, :, c * HEAD : (c + 1) * HEAD] = wide[base * 2 + c, rows].astype(BF16)
            copy = pltpu.make_async_copy(vmem.at[r], out.at[r], sems.at[r, base])
            copy.start()
            copies.append(copy)
    for copy in copies:
        copy.wait()


def place(got, table):
    shape = (2, NEW_CAP, 2 * HEAD)
    out_spec = pl.BlockSpec(memory_space=pltpu.HBM)
    return pl.pallas_call(
        place_kernel,
        in_specs=[pl.BlockSpec(memory_space=pltpu.SMEM), pl.BlockSpec(memory_space=pltpu.VMEM)],
        out_specs=[out_spec, out_spec],
        out_shape=[jax.ShapeDtypeStruct(shape, BF16)] * 2,
        scratch_shapes=[
            pltpu.VMEM((4, 2 * PLACE_ROWS, HEAD), F32),
            pltpu.VMEM(shape, BF16),
            pltpu.VMEM(shape, BF16),
            pltpu.SemaphoreType.DMA((2, 2)),
        ],
        compiler_params=pltpu.CompilerParams(vmem_limit_bytes=16 * 2**20),
        cost_estimate=pl.CostEstimate(flops=10**6, bytes_accessed=4 * 2**20, transcendentals=0),
        name="place_rows",
    )(table, got)


def diagonal():
    rows = lax.broadcasted_iota(jnp.int32, (PART_ROWS, HEAD), 0)
    lanes = lax.broadcasted_iota(jnp.int32, (PART_ROWS, HEAD), 1)
    return rows == lanes


def to_row(column):
    return jnp.sum(jnp.where(diagonal(), column, 0.0), axis=0, keepdims=True)


def to_column(row):
    return jnp.sum(jnp.where(diagonal(), row, 0.0), axis=1, keepdims=True)


def three_terms(x):
    high = x.astype(BF16).astype(F32)
    rest = x - high
    middle = rest.astype(BF16).astype(F32)
    return [high, middle, rest - middle]


def stat_rows(top, total):
    terms = three_terms(top) + three_terms(total)
    index = lax.broadcasted_iota(jnp.int32, (16, HEAD), 0)
    packed = jnp.zeros((16, HEAD), F32)
    for i, term in enumerate(terms):
        packed = jnp.where(index == i, term, packed)
    return packed.astype(BF16)


def read_stats(payload):
    stats = payload[PART_ROWS:PAY_ROWS].astype(F32)
    top = stats[0:1] + stats[1:2] + stats[2:3]
    total = stats[3:4] + stats[4:5] + stats[5:6]
    return top, total


def stack_queries(q, kh):
    heads = [q[:, h * HEAD : (h + 1) * HEAD].astype(F32) for h in range(kh * 8, kh * 8 + 8)]
    return jnp.concatenate(heads, axis=0).astype(BF16)


def partial_of(q, keys, values, allowed):
    x = jnp.where(allowed, nt_dot(q, keys), MASKED)
    top = jnp.max(x, axis=1, keepdims=True)
    weights = jnp.exp2((x - top) * SCALE2).astype(BF16)
    out = nn_dot(weights, jnp.concatenate([values, jnp.ones_like(values)], axis=1))
    return top, out[:, HEAD : HEAD + 1], out[:, :HEAD] / out[:, HEAD:]


def relative_group(step, other):
    group = lax.axis_index("req")
    chip = (lax.shift_right_logical(group, 1) - step) & 3
    return chip * 2 + ((group & 1) ^ other)


def passage_kernel(len_ref, req_ref, *refs):
    query_refs, (k_ref, v_ref), out_refs = refs[:4], refs[4:6], refs[6:]
    sender = my_sender()
    row_request = lax.shift_right_logical(lax.broadcasted_iota(jnp.int32, (64, 1), 0), 2) & 1
    lengths = [len_ref[j, sender] for j in range(PASSAGES)]
    requests = [req_ref[j, sender] for j in range(PASSAGES)]
    for index in range(GROUPS):
        step, other = index // 2, index % 2
        group = relative_group(step, other)
        begin, end, local, reach = jnp.int32(0), jnp.int32(0), jnp.int32(0), jnp.int32(0)
        for length, request in zip(lengths, requests):
            hit = lax.shift_right_logical(request, 1) == group
            begin = jnp.where(hit, reach, begin)
            reach = reach + length
            end = jnp.where(hit, reach, end)
            local = jnp.where(hit, request & 1, local)
        first = pl.multiple_of(jnp.minimum(begin & -TILE, ROWS - WINDOW), TILE)
        keys = first + lax.broadcasted_iota(jnp.int32, (64, WINDOW), 1)
        allowed = (keys >= begin) & (keys < end)
        q = query_refs[step][other]
        tops, totals = [], []
        for kh in range(2):
            lanes = slice(kh * HEAD, (kh + 1) * HEAD)
            top, total, out = partial_of(
                stack_queries(q, kh),
                k_ref[pl.ds(first, WINDOW), lanes],
                v_ref[pl.ds(first, WINDOW), lanes],
                allowed,
            )
            tops.append(jnp.where(row_request == local, top, MASKED))
            totals.append(total)
            out_refs[index][kh * 64 : (kh + 1) * 64] = out.astype(BF16)
        out_refs[index][PART_ROWS:PAY_ROWS] = stat_rows(
            to_row(jnp.concatenate(tops, axis=0)), to_row(jnp.concatenate(totals, axis=0))
        )


def passage_partials(queries, k, v, pass_len, pass_req):
    ins = [*queries, k, v]
    return pl.pallas_call(
        passage_kernel,
        grid_spec=pltpu.PrefetchScalarGridSpec(
            num_scalar_prefetch=2,
            grid=(1,),
            in_specs=[pl.BlockSpec(a.shape, lambda i, n, r, d=a.ndim: (0,) * d) for a in ins],
            out_specs=[pl.BlockSpec((PAY_ROWS, HEAD), lambda i, n, r: (0, 0))] * GROUPS,
        ),
        out_shape=[jax.ShapeDtypeStruct((PAY_ROWS, HEAD), BF16)] * GROUPS,
        compiler_params=pltpu.CompilerParams(vmem_limit_bytes=16 * 2**20),
        cost_estimate=pl.CostEstimate(flops=10**9, bytes_accessed=3 * 2**20, transcendentals=10**6),
        name="passage_partials",
    )(pass_len, pass_req, *ins)


def context_kernel(fill_ref, q_ref, ck_ref, cv_ref, dk_ref, dv_ref, out_ref):
    row_request = lax.shift_right_logical(lax.broadcasted_iota(jnp.int32, (64, 1), 0), 2) & 1
    q = q_ref[...]
    context = ck_ref.shape[1]
    keys = lax.broadcasted_iota(jnp.int32, (64, context), 1)
    own_key = lax.broadcasted_iota(jnp.int32, (64, 8), 1)
    own_row = lax.broadcasted_iota(jnp.int32, (64, 8), 0) & 7
    same = lax.shift_right_logical(own_key, 2) == lax.shift_right_logical(own_row, 2)
    own_allowed = (own_key <= own_row) & same
    stats = [[], [], [], []]
    for kh in range(2):
        lanes = slice(kh * HEAD, (kh + 1) * HEAD)
        queries = stack_queries(q, kh)
        parts = [
            partial_of(queries, ck_ref[r, :, lanes], cv_ref[r, :, lanes], keys < fill_ref[0, r])
            for r in range(2)
        ]
        top, total, out = [jnp.where(row_request == 0, a, b) for a, b in zip(parts[0], parts[1])]
        out_ref[0, kh * 64 : (kh + 1) * 64] = out.astype(BF16)
        stats[0].append(top)
        stats[1].append(total)
        top, total, out = partial_of(queries, dk_ref[:, lanes], dv_ref[:, lanes], own_allowed)
        out_ref[1, kh * 64 : (kh + 1) * 64] = out.astype(BF16)
        stats[2].append(top)
        stats[3].append(total)
    rows = [to_row(jnp.concatenate(s, axis=0)) for s in stats]
    out_ref[0, PART_ROWS:PAY_ROWS] = stat_rows(rows[0], rows[1])
    out_ref[1, PART_ROWS:PAY_ROWS] = stat_rows(rows[2], rows[3])


def context_partials(q, ck, cv, dk, dv, fill):
    ins = [q, ck, cv, dk, dv]
    return pl.pallas_call(
        context_kernel,
        grid_spec=pltpu.PrefetchScalarGridSpec(
            num_scalar_prefetch=1,
            grid=(1,),
            in_specs=[pl.BlockSpec(a.shape, lambda i, f, d=a.ndim: (0,) * d) for a in ins],
            out_specs=pl.BlockSpec((2, PAY_ROWS, HEAD), lambda i, f: (0, 0, 0)),
        ),
        out_shape=jax.ShapeDtypeStruct((2, PAY_ROWS, HEAD), BF16),
        compiler_params=pltpu.CompilerParams(vmem_limit_bytes=16 * 2**20),
        cost_estimate=pl.CostEstimate(flops=10**9, bytes_accessed=3 * 2**20, transcendentals=10**6),
        name="context_partials",
    )(fill, *ins)


def combine(payloads):
    stats = [read_stats(p) for p in payloads]
    joint = functools.reduce(jnp.maximum, [top for top, _ in stats])
    shares = [total * jnp.exp2((top - joint) * SCALE2) for top, total in stats]
    total = functools.reduce(jnp.add, shares)
    out = jnp.zeros((PART_ROWS, HEAD), F32)
    for share, payload in zip(shares, payloads):
        out = out + to_column(share / total) * payload[:PART_ROWS].astype(F32)
    return joint, total, out


def merge_kernel(*refs):
    got_refs, own_ref, out_ref = refs[:GROUPS], refs[GROUPS], refs[GROUPS + 1]
    joint, total, out = combine([ref[...] for ref in got_refs] + [own_ref[0]])
    out_ref[:PART_ROWS] = out.astype(BF16)
    out_ref[PART_ROWS:PAY_ROWS] = stat_rows(joint, total)


def merge(got, own):
    return pl.pallas_call(
        merge_kernel,
        out_shape=jax.ShapeDtypeStruct((PAY_ROWS, HEAD), BF16),
        compiler_params=pltpu.CompilerParams(vmem_limit_bytes=8 * 2**20),
        name="merge_partials",
    )(*got, own)


def finish_kernel(*refs):
    got_refs, own_ref, out_ref = refs[:SHARDS], refs[SHARDS], refs[SHARDS + 1]
    _, _, out = combine([ref[...] for ref in got_refs] + [own_ref[1]])
    for h in range(16):
        out_ref[:, h * HEAD : (h + 1) * HEAD] = out[h * 8 : (h + 1) * 8].astype(BF16)


def finish(got, own):
    return pl.pallas_call(
        finish_kernel,
        out_shape=jax.ShapeDtypeStruct((8, 16 * HEAD), BF16),
        compiler_params=pltpu.CompilerParams(vmem_limit_bytes=8 * 2**20),
        name="finish_decode",
    )(*got, own)


def moved(x, axis, target):
    return lax.ppermute(x, axis, [(i, target(i)) for i in range(8)])


def group_step(i, step, other):
    return ((i // 2 + step) % 4) * 2 + (i % 2 ^ other)


def spread(pair, axis):
    return [pair] + [moved(pair, axis, lambda i, d=d: (i + d) % 8) for d in (2, 4, 6)]


def after(value, other):
    return lax.optimization_barrier((value, other))[0]


def body(
    q_pass,
    k_pass,
    passage_values,
    pass_len,
    pass_req,
    cache_fill,
    cache_k,
    cached_values,
    q_dec,
    decode_keys,
    decode_values,
):
    pass_len, pass_req, cache_fill = pass_len.T, pass_req.T, cache_fill.T
    send = pack(k_pass, passage_values, pass_len, pass_req)
    got = lax.all_to_all(send, ("req", "seq"), split_axis=0, concat_axis=0, tiled=True)
    pair = jnp.stack([q_dec, moved(q_dec, "req", lambda i: i ^ 1)])
    queries = spread(after(pair, send), "req")
    half_out = passage_attention(
        q_pass, k_pass, passage_values, after(pass_len, queries[0]), 0, 5
    )
    to_groups = passage_partials(
        after(queries, half_out), k_pass, passage_values, pass_len, pass_req
    )
    from_groups = [to_groups[0]] + [
        moved(block, "req", lambda i, n=n: group_step(i, -(n // 2), n % 2))
        for n, block in enumerate(to_groups)
        if n > 0
    ]
    own = context_partials(
        q_dec, cache_k, cached_values, decode_keys, decode_values, after(cache_fill, to_groups)
    )
    table = place_table(*after((pass_len, pass_req), to_groups))
    part = merge(after(from_groups, table), own)
    parts = [part] + [moved(part, "seq", lambda i, d=d: (i + d) % 8) for d in (4, 3, 5, 2, 6, 1, 7)]
    pass_out = passage_attention(
        q_pass, k_pass, passage_values, after(pass_len, part), 5, 3, (half_out,)
    )
    new_k, new_v = place(got, table)
    dec_out = finish(after(parts, (pass_out, new_k)), own)
    return (pass_out, new_k, new_v, dec_out)


def solution(mesh):
    placed = (
        P(("req", "seq"), "tp"),
        P(("req", "seq"), "tp"),
        P(("req", "seq"), "tp"),
        P(),
        P(),
        P("req", "seq"),
        P("req", "seq", "tp"),
        P("req", "seq", "tp"),
        P("req", "tp"),
        P("req", "tp"),
        P("req", "tp"),
    )
    return jax.shard_map(
        body,
        mesh=mesh,
        in_specs=placed,
        out_specs=(
            P(("req", "seq"), "tp"),
            P("req", "seq", "tp"),
            P("req", "seq", "tp"),
            P("req", "tp"),
        ),
        check_vma=False,
    )
```

```python
import functools
import math

import jax
import jax.numpy as jnp
from jax import lax
from jax.experimental import pallas as pl
from jax.experimental.pallas import tpu as pltpu
from jax.sharding import PartitionSpec as P

HEAD = 128
TILE = 128
SHARDS = 8
GROUPS = 8
PASSAGES = 8
SLOT_CAP = 32
HALF_CAP = 16
NEW_CAP = 1024
ROWS = 1024
PLACE_ROWS = NEW_CAP + SLOT_CAP
MASKED = -1e30
SCALE2 = HEAD**-0.5 * math.log2(math.e)
PART_ROWS = 128
PAY_ROWS = 144
WINDOW = 384
ATTN_VMEM = 24 * 2**20
BF16 = jnp.bfloat16
F32 = jnp.float32


def nt_dot(a, b):
    return lax.dot_general(a, b, (((1,), (1,)), ((), ())), preferred_element_type=F32)


def nn_dot(a, b):
    return lax.dot_general(a, b, (((1,), (0,)), ((), ())), preferred_element_type=F32)


def my_sender():
    return lax.axis_index("req") * SHARDS + lax.axis_index("seq")


def attn_kernel(first_tile, len_ref, q_ref, k_ref, v_ref, *refs):
    o_ref = refs[-1]
    sender = my_sender()
    row0 = (pl.program_id(0) + first_tile) * TILE
    starts = [jnp.int32(0)]
    for j in range(PASSAGES - 1):
        starts.append(starts[-1] + len_ref[j, sender])
    first = jnp.int32(0)
    for start in starts[1:]:
        first = jnp.where(start <= row0, start, first)

    def work(tiles):
        width = tiles * TILE
        key0 = pl.multiple_of(row0 - (tiles - 1) * TILE, TILE)
        rows = row0 + lax.broadcasted_iota(jnp.int32, (TILE, width), 0)
        keys = key0 + lax.broadcasted_iota(jnp.int32, (TILE, width), 1)
        begin = jnp.zeros((TILE, width), jnp.int32)
        for start in starts[1:]:
            begin = jnp.where(rows >= start, start, begin)
        allowed = (keys >= begin) & (keys <= rows)
        for kh in range(2):
            lanes = slice(kh * HEAD, (kh + 1) * HEAD)
            keys_block = k_ref[pl.ds(key0, width), lanes]
            values = v_ref[pl.ds(key0, width), lanes]
            values = jnp.concatenate([values, jnp.ones_like(values)], axis=1)
            heads = range(kh * 8, kh * 8 + 8)
            q = jnp.concatenate([q_ref[:, h * HEAD : (h + 1) * HEAD] for h in heads], axis=0)
            scores = nt_dot(q, keys_block)
            weights = []
            for t in range(8):
                x = jnp.where(allowed, scores[t * TILE : (t + 1) * TILE], MASKED)
                top = jnp.max(x, axis=1, keepdims=True)
                weights.append(jnp.exp2((x - top) * SCALE2).astype(BF16))
            out = nn_dot(jnp.concatenate(weights, axis=0), values)
            for t, h in enumerate(heads):
                part = out[t * TILE : (t + 1) * TILE]
                o_ref[:, h * HEAD : (h + 1) * HEAD] = (part[:, :HEAD] / part[:, HEAD:]).astype(BF16)

    one = first >= row0
    two = first >= row0 - TILE

    @pl.when(one)
    def _():
        work(1)

    @pl.when(jnp.logical_and(jnp.logical_not(one), two))
    def _():
        work(2)

    @pl.when(jnp.logical_not(two))
    def _():
        work(3)


def passage_attention(q, k, v, pass_len, first_tile, tiles, earlier=()):
    tile_spec = pl.BlockSpec((TILE, q.shape[1]), lambda i, n: (i + first_tile, 0))
    return pl.pallas_call(
        functools.partial(attn_kernel, first_tile),
        grid_spec=pltpu.PrefetchScalarGridSpec(
            num_scalar_prefetch=1,
            grid=(tiles,),
            in_specs=[
                tile_spec,
                pl.BlockSpec(k.shape, lambda i, n: (0, 0)),
                pl.BlockSpec(v.shape, lambda i, n: (0, 0)),
            ]
            + [pl.BlockSpec(memory_space=pltpu.HBM) for _ in earlier],
            out_specs=tile_spec,
        ),
        out_shape=jax.ShapeDtypeStruct(q.shape, q.dtype),
        input_output_aliases={4: 0} if earlier else {},
        compiler_params=pltpu.CompilerParams(vmem_limit_bytes=ATTN_VMEM),
        cost_estimate=pl.CostEstimate(
            flops=10**9 * tiles, bytes_accessed=2**20 * tiles, transcendentals=10**6 * tiles
        ),
        name="passage_attention",
    )(pass_len, q, k, v, *earlier)


def pack_kernel(len_any, req_any, k_any, v_any, out_any, len_ref, req_ref, k_ref, v_ref, wide, packed, sems):
    copies = [
        pltpu.make_async_copy(source, target, sems.at[i])
        for i, (source, target) in enumerate(
            [(len_any, len_ref), (req_any, req_ref), (k_any, k_ref), (v_any, v_ref)]
        )
    ]
    for i in (2, 3, 0, 1):
        copies[i].start()
    sender = my_sender()
    for i, rows in ((0, k_ref), (1, v_ref)):
        copies[2 + i].wait()
        for c in range(2):
            wide[2 * i + c, :ROWS] = rows[:, c * HEAD : (c + 1) * HEAD].astype(F32)
    copies[0].wait()
    copies[1].wait()

    def gather(j, begin, half):
        for residue in range(SHARDS):
            lead = lax.shift_right_logical(begin + (7 - residue), 3) + half * HALF_CAP
            for c in range(4):
                rows = wide[c, pl.ds(lead * 8 + residue, HALF_CAP, stride=8), :]
                packed[j, residue, half * HALF_CAP : (half + 1) * HALF_CAP, c * HEAD : (c + 1) * HEAD] = rows.astype(BF16)

    def send(j, half):
        group = lax.shift_right_logical(req_ref[j, sender], 1)
        rows = pl.ds(half * HALF_CAP, HALF_CAP)
        return pltpu.make_async_copy(
            packed.at[j, :, rows], out_any.at[pl.ds(group * SHARDS, SHARDS), rows], sems.at[4 + 2 * j + half]
        )

    begin = jnp.int32(0)
    for j in range(PASSAGES):
        gather(j, begin, 0)
        send(j, 0).start()

        @pl.when(len_ref[j, sender] > HALF_CAP * SHARDS)
        def _():
            gather(j, begin, 1)
            send(j, 1).start()

        begin = begin + len_ref[j, sender]
    for j in range(PASSAGES):
        send(j, 0).wait()

        @pl.when(len_ref[j, sender] > HALF_CAP * SHARDS)
        def _():
            send(j, 1).wait()


def pack(k, v, pass_len, pass_req):
    anywhere = pl.BlockSpec(memory_space=pltpu.HBM)
    return pl.pallas_call(
        pack_kernel,
        in_specs=[anywhere] * 4,
        out_specs=anywhere,
        out_shape=jax.ShapeDtypeStruct((64, SLOT_CAP, 4 * HEAD), BF16),
        scratch_shapes=[
            pltpu.SMEM(pass_len.shape, jnp.int32),
            pltpu.SMEM(pass_req.shape, jnp.int32),
            pltpu.VMEM(k.shape, BF16),
            pltpu.VMEM(v.shape, BF16),
            pltpu.VMEM((4, ROWS + 256, HEAD), F32),
            pltpu.VMEM((PASSAGES, SHARDS, SLOT_CAP, 4 * HEAD), BF16),
            pltpu.SemaphoreType.DMA((4 + 2 * PASSAGES,)),
        ],
        compiler_params=pltpu.CompilerParams(vmem_limit_bytes=60 * 2**20),
        cost_estimate=pl.CostEstimate(flops=10**6, bytes_accessed=3 * 2**20, transcendentals=0),
        name="pack_rows",
    )(pass_len, pass_req, k, v)


def fill_table(len_ref, req_ref, out_ref):
    group = lax.axis_index("req")
    shard = lax.axis_index("seq")
    begin = start = length = local = jnp.zeros((1, 64), jnp.int32)
    for j in range(PASSAGES):
        rows = len_ref[j : j + 1, :]
        request = req_ref[j : j + 1, :]
        hit = lax.shift_right_logical(request, 1) == group
        start = jnp.where(hit, begin, start)
        length = jnp.where(hit, rows, length)
        local = jnp.where(hit, request & 1, local)
        begin = begin + rows
    lead = lax.shift_right_logical(start + (7 - shard), 3)
    count = lax.shift_right_logical(start + length + (7 - shard), 3) - lead
    index = lax.broadcasted_iota(jnp.int32, (8, 64), 0)
    counts = jnp.where(index == 1, jnp.where(local == 0, count, 0), 0)
    counts = jnp.where(index == 2, jnp.where(local == 0, 0, count), counts)
    counts = jnp.where(index == 0, count, counts).astype(F32).astype(BF16)
    source = lax.broadcasted_iota(jnp.int32, (64, 128), 0)
    lane = lax.broadcasted_iota(jnp.int32, (64, 128), 1)
    before = nn_dot(counts, jnp.where(source < lane, 1.0, 0.0).astype(BF16)).astype(jnp.int32)
    out_ref[...] = before
    out_ref[0:1, 0:64] = jnp.where(local == 0, before[1:2, 0:64], PLACE_ROWS + before[2:3, 0:64])


def place_kernel(table_ref, got_ref, k_any, v_any, wide, k_ref, v_ref, sems):
    def one_sender(source, carry):
        row = table_ref[0, source]
        for c in range(4):
            block = got_ref[source, :, c * HEAD : (c + 1) * HEAD].astype(F32)
            wide[c, pl.ds(row, SLOT_CAP), :] = block
        return carry

    lax.fori_loop(0, 64, one_sender, 0, unroll=4)
    copies = []
    for r in range(2):
        filled = table_ref[1 + r, 64]

        def clear(i, carry):
            for c in range(4):
                wide[c, pl.ds(r * PLACE_ROWS + filled + i * SLOT_CAP, SLOT_CAP), :] = jnp.zeros((SLOT_CAP, HEAD), F32)
            return carry

        lax.fori_loop(0, lax.shift_right_logical(NEW_CAP - filled + SLOT_CAP - 1, 5), clear, 0)
        rows = slice(r * PLACE_ROWS, r * PLACE_ROWS + NEW_CAP)
        for base, (vmem, out) in enumerate(((k_ref, k_any), (v_ref, v_any))):
            for c in range(2):
                vmem[r, :, c * HEAD : (c + 1) * HEAD] = wide[base * 2 + c, rows].astype(BF16)
            copy = pltpu.make_async_copy(vmem.at[r], out.at[r], sems.at[r, base])
            copy.start()
            copies.append(copy)
    for copy in copies:
        copy.wait()


def place(got, table):
    shape = (2, NEW_CAP, 2 * HEAD)
    out_spec = pl.BlockSpec(memory_space=pltpu.HBM)
    return pl.pallas_call(
        place_kernel,
        in_specs=[pl.BlockSpec(memory_space=pltpu.SMEM), pl.BlockSpec(memory_space=pltpu.VMEM)],
        out_specs=[out_spec, out_spec],
        out_shape=[jax.ShapeDtypeStruct(shape, BF16)] * 2,
        scratch_shapes=[
            pltpu.VMEM((4, 2 * PLACE_ROWS, HEAD), F32),
            pltpu.VMEM(shape, BF16),
            pltpu.VMEM(shape, BF16),
            pltpu.SemaphoreType.DMA((2, 2)),
        ],
        compiler_params=pltpu.CompilerParams(vmem_limit_bytes=16 * 2**20),
        cost_estimate=pl.CostEstimate(flops=10**6, bytes_accessed=4 * 2**20, transcendentals=0),
        name="place_rows",
    )(table, got)


def diagonal():
    rows = lax.broadcasted_iota(jnp.int32, (PART_ROWS, HEAD), 0)
    lanes = lax.broadcasted_iota(jnp.int32, (PART_ROWS, HEAD), 1)
    return rows == lanes


def to_row(column):
    return jnp.sum(jnp.where(diagonal(), column, 0.0), axis=0, keepdims=True)


def to_column(row):
    return jnp.sum(jnp.where(diagonal(), row, 0.0), axis=1, keepdims=True)


def three_terms(x):
    high = x.astype(BF16).astype(F32)
    rest = x - high
    middle = rest.astype(BF16).astype(F32)
    return [high, middle, rest - middle]


def stat_rows(top, total):
    terms = three_terms(top) + three_terms(total)
    index = lax.broadcasted_iota(jnp.int32, (16, HEAD), 0)
    packed = jnp.zeros((16, HEAD), F32)
    for i, term in enumerate(terms):
        packed = jnp.where(index == i, term, packed)
    return packed.astype(BF16)


def read_stats(payload):
    stats = payload[PART_ROWS:PAY_ROWS].astype(F32)
    top = stats[0:1] + stats[1:2] + stats[2:3]
    total = stats[3:4] + stats[4:5] + stats[5:6]
    return top, total


def stack_queries(q, kh):
    heads = [q[:, h * HEAD : (h + 1) * HEAD].astype(F32) for h in range(kh * 8, kh * 8 + 8)]
    return jnp.concatenate(heads, axis=0).astype(BF16)


def partial_of(q, keys, values, allowed):
    x = jnp.where(allowed, nt_dot(q, keys), MASKED)
    top = jnp.max(x, axis=1, keepdims=True)
    weights = jnp.exp2((x - top) * SCALE2).astype(BF16)
    out = nn_dot(weights, jnp.concatenate([values, jnp.ones_like(values)], axis=1))
    return top, out[:, HEAD : HEAD + 1], out[:, :HEAD] / out[:, HEAD:]


def relative_group(step, other):
    group = lax.axis_index("req")
    chip = (lax.shift_right_logical(group, 1) - step) & 3
    return chip * 2 + ((group & 1) ^ other)


def passage_kernel(len_ref, req_ref, *refs):
    query_refs, (k_ref, v_ref), out_refs = refs[:4], refs[4:6], refs[6:]
    sender = my_sender()
    row_request = lax.shift_right_logical(lax.broadcasted_iota(jnp.int32, (64, 1), 0), 2) & 1
    lengths = [len_ref[j, sender] for j in range(PASSAGES)]
    requests = [req_ref[j, sender] for j in range(PASSAGES)]
    for index in range(GROUPS):
        step, other = index // 2, index % 2
        group = relative_group(step, other)
        begin, end, local, reach = jnp.int32(0), jnp.int32(0), jnp.int32(0), jnp.int32(0)
        for length, request in zip(lengths, requests):
            hit = lax.shift_right_logical(request, 1) == group
            begin = jnp.where(hit, reach, begin)
            reach = reach + length
            end = jnp.where(hit, reach, end)
            local = jnp.where(hit, request & 1, local)
        first = pl.multiple_of(jnp.minimum(begin & -TILE, ROWS - WINDOW), TILE)
        keys = first + lax.broadcasted_iota(jnp.int32, (64, WINDOW), 1)
        allowed = (keys >= begin) & (keys < end)
        q = query_refs[step][other]
        tops, totals = [], []
        for kh in range(2):
            lanes = slice(kh * HEAD, (kh + 1) * HEAD)
            top, total, out = partial_of(
                stack_queries(q, kh),
                k_ref[pl.ds(first, WINDOW), lanes],
                v_ref[pl.ds(first, WINDOW), lanes],
                allowed,
            )
            tops.append(jnp.where(row_request == local, top, MASKED))
            totals.append(total)
            out_refs[index][kh * 64 : (kh + 1) * 64] = out.astype(BF16)
        out_refs[index][PART_ROWS:PAY_ROWS] = stat_rows(
            to_row(jnp.concatenate(tops, axis=0)), to_row(jnp.concatenate(totals, axis=0))
        )


def passage_partials(queries, k, v, pass_len, pass_req):
    ins = [*queries, k, v]
    return pl.pallas_call(
        passage_kernel,
        grid_spec=pltpu.PrefetchScalarGridSpec(
            num_scalar_prefetch=2,
            grid=(1,),
            in_specs=[pl.BlockSpec(a.shape, lambda i, n, r, d=a.ndim: (0,) * d) for a in ins],
            out_specs=[pl.BlockSpec((PAY_ROWS, HEAD), lambda i, n, r: (0, 0))] * GROUPS,
        ),
        out_shape=[jax.ShapeDtypeStruct((PAY_ROWS, HEAD), BF16)] * GROUPS,
        compiler_params=pltpu.CompilerParams(vmem_limit_bytes=16 * 2**20),
        cost_estimate=pl.CostEstimate(flops=10**9, bytes_accessed=3 * 2**20, transcendentals=10**6),
        name="passage_partials",
    )(pass_len, pass_req, *ins)


def context_kernel(fill_ref, len_ref, req_ref, q_ref, ck_ref, cv_ref, dk_ref, dv_ref, out_ref, table_ref):
    fill_table(len_ref, req_ref, table_ref)
    row_request = lax.shift_right_logical(lax.broadcasted_iota(jnp.int32, (64, 1), 0), 2) & 1
    q = q_ref[...]
    context = ck_ref.shape[1]
    keys = lax.broadcasted_iota(jnp.int32, (64, context), 1)
    own_key = lax.broadcasted_iota(jnp.int32, (64, 8), 1)
    own_row = lax.broadcasted_iota(jnp.int32, (64, 8), 0) & 7
    same = lax.shift_right_logical(own_key, 2) == lax.shift_right_logical(own_row, 2)
    own_allowed = (own_key <= own_row) & same
    stats = [[], [], [], []]
    for kh in range(2):
        lanes = slice(kh * HEAD, (kh + 1) * HEAD)
        queries = stack_queries(q, kh)
        parts = [
            partial_of(queries, ck_ref[r, :, lanes], cv_ref[r, :, lanes], keys < fill_ref[0, r])
            for r in range(2)
        ]
        top, total, out = [jnp.where(row_request == 0, a, b) for a, b in zip(parts[0], parts[1])]
        out_ref[0, kh * 64 : (kh + 1) * 64] = out.astype(BF16)
        stats[0].append(top)
        stats[1].append(total)
        top, total, out = partial_of(queries, dk_ref[:, lanes], dv_ref[:, lanes], own_allowed)
        out_ref[1, kh * 64 : (kh + 1) * 64] = out.astype(BF16)
        stats[2].append(top)
        stats[3].append(total)
    rows = [to_row(jnp.concatenate(s, axis=0)) for s in stats]
    out_ref[0, PART_ROWS:PAY_ROWS] = stat_rows(rows[0], rows[1])
    out_ref[1, PART_ROWS:PAY_ROWS] = stat_rows(rows[2], rows[3])


def context_partials(q, ck, cv, dk, dv, pass_len, pass_req, fill):
    ins = [pass_len, pass_req, q, ck, cv, dk, dv]
    return pl.pallas_call(
        context_kernel,
        grid_spec=pltpu.PrefetchScalarGridSpec(
            num_scalar_prefetch=1,
            grid=(1,),
            in_specs=[pl.BlockSpec(a.shape, lambda i, f, d=a.ndim: (0,) * d) for a in ins],
            out_specs=[
                pl.BlockSpec((2, PAY_ROWS, HEAD), lambda i, f: (0, 0, 0)),
                pl.BlockSpec((8, 128), lambda i, f: (0, 0)),
            ],
        ),
        out_shape=[
            jax.ShapeDtypeStruct((2, PAY_ROWS, HEAD), BF16),
            jax.ShapeDtypeStruct((8, 128), jnp.int32),
        ],
        compiler_params=pltpu.CompilerParams(vmem_limit_bytes=16 * 2**20),
        cost_estimate=pl.CostEstimate(flops=10**9, bytes_accessed=3 * 2**20, transcendentals=10**6),
        name="context_partials",
    )(fill, *ins)


def combine(payloads):
    stats = [read_stats(p) for p in payloads]
    joint = functools.reduce(jnp.maximum, [top for top, _ in stats])
    shares = [total * jnp.exp2((top - joint) * SCALE2) for top, total in stats]
    total = functools.reduce(jnp.add, shares)
    out = jnp.zeros((PART_ROWS, HEAD), F32)
    for share, payload in zip(shares, payloads):
        out = out + to_column(share / total) * payload[:PART_ROWS].astype(F32)
    return joint, total, out


def merge_kernel(*refs):
    got_refs, own_ref, out_ref = refs[:GROUPS], refs[GROUPS], refs[GROUPS + 1]
    joint, total, out = combine([ref[...] for ref in got_refs] + [own_ref[0]])
    out_ref[:PART_ROWS] = out.astype(BF16)
    out_ref[PART_ROWS:PAY_ROWS] = stat_rows(joint, total)


def merge(got, own):
    return pl.pallas_call(
        merge_kernel,
        out_shape=jax.ShapeDtypeStruct((PAY_ROWS, HEAD), BF16),
        compiler_params=pltpu.CompilerParams(vmem_limit_bytes=8 * 2**20),
        name="merge_partials",
    )(*got, own)


def finish_kernel(*refs):
    got_refs, own_ref, out_ref = refs[:SHARDS], refs[SHARDS], refs[SHARDS + 1]
    _, _, out = combine([ref[...] for ref in got_refs] + [own_ref[1]])
    for h in range(16):
        out_ref[:, h * HEAD : (h + 1) * HEAD] = out[h * 8 : (h + 1) * 8].astype(BF16)


def finish(got, own):
    return pl.pallas_call(
        finish_kernel,
        out_shape=jax.ShapeDtypeStruct((8, 16 * HEAD), BF16),
        compiler_params=pltpu.CompilerParams(vmem_limit_bytes=8 * 2**20),
        name="finish_decode",
    )(*got, own)


def moved(x, axis, target):
    return lax.ppermute(x, axis, [(i, target(i)) for i in range(8)])


def shifted(x, d):
    return moved(x, "seq", lambda i: (i + d) % 8)


def group_step(i, step, other):
    return ((i // 2 + step) % 4) * 2 + (i % 2 ^ other)


def spread(pair, axis):
    return [pair] + [moved(pair, axis, lambda i, d=d: (i + d) % 8) for d in (2, 4, 6)]


def after(value, other):
    return lax.optimization_barrier((value, other))[0]


def body(
    q_pass,
    k_pass,
    passage_values,
    pass_len,
    pass_req,
    cache_fill,
    cache_k,
    cached_values,
    q_dec,
    decode_keys,
    decode_values,
):
    pass_len, pass_req, cache_fill = pass_len.T, pass_req.T, cache_fill.T
    peer = moved(q_dec, "req", lambda i: i ^ 1)
    send = after(pack(k_pass, passage_values, pass_len, pass_req), peer)
    got = lax.all_to_all(send, ("req", "seq"), split_axis=0, concat_axis=0, tiled=True)
    queries = spread(after(jnp.stack([q_dec, peer]), send), "req")
    half_out = passage_attention(
        q_pass, k_pass, passage_values, after(pass_len, queries[0]), 0, 5
    )
    to_groups = passage_partials(
        after(queries, half_out), k_pass, passage_values, pass_len, pass_req
    )
    from_groups = [to_groups[0]] + [
        moved(block, "req", lambda i, n=n: group_step(i, -(n // 2), n % 2))
        for n, block in enumerate(to_groups)
        if n > 0
    ]
    own, table = context_partials(
        q_dec,
        cache_k,
        cached_values,
        decode_keys,
        decode_values,
        pass_len,
        pass_req,
        after(cache_fill, to_groups),
    )
    pass_out = passage_attention(
        q_pass, k_pass, passage_values, after(pass_len, own), 5, 3, (half_out,)
    )
    part = merge(after(from_groups, pass_out), own)
    far = [shifted(part, d) for d in (5, 3, 4)]
    near = [shifted(part, d) for d in (1, 7)]
    parts = [part] + far + near + [shifted(x, d) for x, d in zip(near, (1, 7))]
    new_k, new_v = place(got, table)
    dec_out = finish(after(parts, new_k), own)
    return (pass_out, new_k, new_v, dec_out)


def solution(mesh):
    placed = (
        P(("req", "seq"), "tp"),
        P(("req", "seq"), "tp"),
        P(("req", "seq"), "tp"),
        P(),
        P(),
        P("req", "seq"),
        P("req", "seq", "tp"),
        P("req", "seq", "tp"),
        P("req", "tp"),
        P("req", "tp"),
        P("req", "tp"),
    )
    return jax.shard_map(
        body,
        mesh=mesh,
        in_specs=placed,
        out_specs=(
            P(("req", "seq"), "tp"),
            P("req", "seq", "tp"),
            P("req", "seq", "tp"),
            P("req", "tp"),
        ),
        check_vma=False,
    )
```

```python
import functools
import math

import jax
import jax.numpy as jnp
from jax import lax
from jax.experimental import pallas as pl
from jax.experimental.pallas import tpu as pltpu
from jax.sharding import PartitionSpec as P

HEAD = 128
TILE = 128
SHARDS = 8
GROUPS = 8
PASSAGES = 8
SLOT_CAP = 32
HALF_CAP = 16
CHUNK = 256
NEW_CAP = 1024
ROWS = 1024
PLACE_ROWS = NEW_CAP + SLOT_CAP
MASKED = -1e30
SCALE2 = HEAD**-0.5 * math.log2(math.e)
PART_ROWS = 128
PAY_ROWS = 144
WINDOW = 384
ATTN_VMEM = 24 * 2**20
BF16 = jnp.bfloat16
F32 = jnp.float32


def nt_dot(a, b):
    return lax.dot_general(a, b, (((1,), (1,)), ((), ())), preferred_element_type=F32)


def nn_dot(a, b):
    return lax.dot_general(a, b, (((1,), (0,)), ((), ())), preferred_element_type=F32)


def my_sender():
    return lax.axis_index("req") * SHARDS + lax.axis_index("seq")


def attn_kernel(first_tile, len_ref, q_ref, k_ref, v_ref, *refs):
    o_ref = refs[-1]
    sender = my_sender()
    row0 = (pl.program_id(0) + first_tile) * TILE
    starts = [jnp.int32(0)]
    for j in range(PASSAGES - 1):
        starts.append(starts[-1] + len_ref[j, sender])
    first = jnp.int32(0)
    for start in starts[1:]:
        first = jnp.where(start <= row0, start, first)

    def work(tiles):
        width = tiles * TILE
        key0 = pl.multiple_of(row0 - (tiles - 1) * TILE, TILE)
        rows = row0 + lax.broadcasted_iota(jnp.int32, (TILE, width), 0)
        keys = key0 + lax.broadcasted_iota(jnp.int32, (TILE, width), 1)
        begin = jnp.zeros((TILE, width), jnp.int32)
        for start in starts[1:]:
            begin = jnp.where(rows >= start, start, begin)
        allowed = (keys >= begin) & (keys <= rows)
        for kh in range(2):
            lanes = slice(kh * HEAD, (kh + 1) * HEAD)
            keys_block = k_ref[pl.ds(key0, width), lanes]
            values = v_ref[pl.ds(key0, width), lanes]
            values = jnp.concatenate([values, jnp.ones_like(values)], axis=1)
            heads = range(kh * 8, kh * 8 + 8)
            q = jnp.concatenate([q_ref[:, h * HEAD : (h + 1) * HEAD] for h in heads], axis=0)
            scores = nt_dot(q, keys_block)
            weights = []
            for t in range(8):
                x = jnp.where(allowed, scores[t * TILE : (t + 1) * TILE], MASKED)
                top = jnp.max(x, axis=1, keepdims=True)
                weights.append(jnp.exp2((x - top) * SCALE2).astype(BF16))
            out = nn_dot(jnp.concatenate(weights, axis=0), values)
            for t, h in enumerate(heads):
                part = out[t * TILE : (t + 1) * TILE]
                o_ref[:, h * HEAD : (h + 1) * HEAD] = (part[:, :HEAD] / part[:, HEAD:]).astype(BF16)

    one = first >= row0
    two = first >= row0 - TILE

    @pl.when(one)
    def _():
        work(1)

    @pl.when(jnp.logical_and(jnp.logical_not(one), two))
    def _():
        work(2)

    @pl.when(jnp.logical_not(two))
    def _():
        work(3)


def passage_attention(q, k, v, pass_len, first_tile, tiles, earlier=()):
    tile_spec = pl.BlockSpec((TILE, q.shape[1]), lambda i, n: (i + first_tile, 0))
    return pl.pallas_call(
        functools.partial(attn_kernel, first_tile),
        grid_spec=pltpu.PrefetchScalarGridSpec(
            num_scalar_prefetch=1,
            grid=(tiles,),
            in_specs=[
                tile_spec,
                pl.BlockSpec(k.shape, lambda i, n: (0, 0)),
                pl.BlockSpec(v.shape, lambda i, n: (0, 0)),
            ]
            + [pl.BlockSpec(memory_space=pltpu.HBM) for _ in earlier],
            out_specs=tile_spec,
        ),
        out_shape=jax.ShapeDtypeStruct(q.shape, q.dtype),
        input_output_aliases={4: 0} if earlier else {},
        compiler_params=pltpu.CompilerParams(vmem_limit_bytes=ATTN_VMEM),
        cost_estimate=pl.CostEstimate(
            flops=10**9 * tiles, bytes_accessed=2**20 * tiles, transcendentals=10**6 * tiles
        ),
        name="passage_attention",
    )(pass_len, q, k, v, *earlier)


def pack_kernel(len_any, req_any, k_any, v_any, out_any, len_ref, req_ref, k_ref, v_ref, wide, packed, sems):
    tables = [
        pltpu.make_async_copy(source, target, sems.at[i])
        for i, (source, target) in enumerate([(len_any, len_ref), (req_any, req_ref)])
    ]
    chunks = [
        [
            pltpu.make_async_copy(source.at[rows], target.at[rows], sems.at[2 + 2 * n + i])
            for i, (source, target) in enumerate([(k_any, k_ref), (v_any, v_ref)])
        ]
        for n, rows in enumerate(pl.ds(n * CHUNK, CHUNK) for n in range(ROWS // CHUNK))
    ]
    for copy in chunks[0] + tables + chunks[1] + chunks[2] + chunks[3]:
        copy.start()
    sender = my_sender()
    for copy in tables:
        copy.wait()

    def widen(n):
        rows = slice(n * CHUNK, (n + 1) * CHUNK)
        for i, ref in enumerate((k_ref, v_ref)):
            chunks[n][i].wait()
            for c in range(2):
                wide[2 * i + c, rows] = ref[rows, c * HEAD : (c + 1) * HEAD].astype(F32)

    def gather(j, begin, half):
        for residue in range(SHARDS):
            lead = lax.shift_right_logical(begin + (7 - residue), 3) + half * HALF_CAP
            for c in range(4):
                rows = wide[c, pl.ds(lead * 8 + residue, HALF_CAP, stride=8), :]
                packed[j, residue, half * HALF_CAP : (half + 1) * HALF_CAP, c * HEAD : (c + 1) * HEAD] = rows.astype(BF16)

    def send(j, half):
        group = lax.shift_right_logical(req_ref[j, sender], 1)
        rows = pl.ds(half * HALF_CAP, HALF_CAP)
        return pltpu.make_async_copy(
            packed.at[j, :, rows], out_any.at[pl.ds(group * SHARDS, SHARDS), rows], sems.at[10 + 2 * j + half]
        )

    begin = jnp.int32(0)
    for j in range(PASSAGES):
        if j < len(chunks):
            widen(j)
        gather(j, begin, 0)
        send(j, 0).start()

        @pl.when(len_ref[j, sender] > HALF_CAP * SHARDS)
        def _():
            gather(j, begin, 1)
            send(j, 1).start()

        begin = begin + len_ref[j, sender]
    for j in range(PASSAGES):
        send(j, 0).wait()

        @pl.when(len_ref[j, sender] > HALF_CAP * SHARDS)
        def _():
            send(j, 1).wait()


def pack(k, v, pass_len, pass_req):
    anywhere = pl.BlockSpec(memory_space=pltpu.HBM)
    return pl.pallas_call(
        pack_kernel,
        in_specs=[anywhere] * 4,
        out_specs=anywhere,
        out_shape=jax.ShapeDtypeStruct((64, SLOT_CAP, 4 * HEAD), BF16),
        scratch_shapes=[
            pltpu.SMEM(pass_len.shape, jnp.int32),
            pltpu.SMEM(pass_req.shape, jnp.int32),
            pltpu.VMEM(k.shape, BF16),
            pltpu.VMEM(v.shape, BF16),
            pltpu.VMEM((4, ROWS + 256, HEAD), F32),
            pltpu.VMEM((PASSAGES, SHARDS, SLOT_CAP, 4 * HEAD), BF16),
            pltpu.SemaphoreType.DMA((10 + 2 * PASSAGES,)),
        ],
        compiler_params=pltpu.CompilerParams(vmem_limit_bytes=60 * 2**20),
        cost_estimate=pl.CostEstimate(flops=10**6, bytes_accessed=3 * 2**20, transcendentals=0),
        name="pack_rows",
    )(pass_len, pass_req, k, v)


def fill_table(len_ref, req_ref, out_ref):
    group = lax.axis_index("req")
    shard = lax.axis_index("seq")
    begin = start = length = local = jnp.zeros((1, 64), jnp.int32)
    for j in range(PASSAGES):
        rows = len_ref[j : j + 1, :]
        request = req_ref[j : j + 1, :]
        hit = lax.shift_right_logical(request, 1) == group
        start = jnp.where(hit, begin, start)
        length = jnp.where(hit, rows, length)
        local = jnp.where(hit, request & 1, local)
        begin = begin + rows
    lead = lax.shift_right_logical(start + (7 - shard), 3)
    count = lax.shift_right_logical(start + length + (7 - shard), 3) - lead
    index = lax.broadcasted_iota(jnp.int32, (8, 64), 0)
    counts = jnp.where(index == 1, jnp.where(local == 0, count, 0), 0)
    counts = jnp.where(index == 2, jnp.where(local == 0, 0, count), counts)
    counts = jnp.where(index == 0, count, counts).astype(F32).astype(BF16)
    source = lax.broadcasted_iota(jnp.int32, (64, 128), 0)
    lane = lax.broadcasted_iota(jnp.int32, (64, 128), 1)
    before = nn_dot(counts, jnp.where(source < lane, 1.0, 0.0).astype(BF16)).astype(jnp.int32)
    out_ref[...] = before
    out_ref[0:1, 0:64] = jnp.where(local == 0, before[1:2, 0:64], PLACE_ROWS + before[2:3, 0:64])


def place_kernel(table_ref, got_ref, k_any, v_any, wide, k_ref, v_ref, sems):
    def one_sender(source, carry):
        row = table_ref[0, source]
        for c in range(4):
            block = got_ref[source, :, c * HEAD : (c + 1) * HEAD].astype(F32)
            wide[c, pl.ds(row, SLOT_CAP), :] = block
        return carry

    lax.fori_loop(0, 64, one_sender, 0, unroll=4)
    copies = []
    for r in range(2):
        filled = table_ref[1 + r, 64]

        def clear(i, carry):
            for c in range(4):
                wide[c, pl.ds(r * PLACE_ROWS + filled + i * SLOT_CAP, SLOT_CAP), :] = jnp.zeros((SLOT_CAP, HEAD), F32)
            return carry

        lax.fori_loop(0, lax.shift_right_logical(NEW_CAP - filled + SLOT_CAP - 1, 5), clear, 0)
        rows = slice(r * PLACE_ROWS, r * PLACE_ROWS + NEW_CAP)
        for base, (vmem, out) in enumerate(((k_ref, k_any), (v_ref, v_any))):
            for c in range(2):
                vmem[r, :, c * HEAD : (c + 1) * HEAD] = wide[base * 2 + c, rows].astype(BF16)
            copy = pltpu.make_async_copy(vmem.at[r], out.at[r], sems.at[r, base])
            copy.start()
            copies.append(copy)
    for copy in copies:
        copy.wait()


def place(got, table):
    shape = (2, NEW_CAP, 2 * HEAD)
    out_spec = pl.BlockSpec(memory_space=pltpu.HBM)
    return pl.pallas_call(
        place_kernel,
        in_specs=[pl.BlockSpec(memory_space=pltpu.SMEM), pl.BlockSpec(memory_space=pltpu.VMEM)],
        out_specs=[out_spec, out_spec],
        out_shape=[jax.ShapeDtypeStruct(shape, BF16)] * 2,
        scratch_shapes=[
            pltpu.VMEM((4, 2 * PLACE_ROWS, HEAD), F32),
            pltpu.VMEM(shape, BF16),
            pltpu.VMEM(shape, BF16),
            pltpu.SemaphoreType.DMA((2, 2)),
        ],
        compiler_params=pltpu.CompilerParams(vmem_limit_bytes=16 * 2**20),
        cost_estimate=pl.CostEstimate(flops=10**6, bytes_accessed=4 * 2**20, transcendentals=0),
        name="place_rows",
    )(table, got)


def diagonal():
    rows = lax.broadcasted_iota(jnp.int32, (PART_ROWS, HEAD), 0)
    lanes = lax.broadcasted_iota(jnp.int32, (PART_ROWS, HEAD), 1)
    return rows == lanes


def to_row(column):
    return jnp.sum(jnp.where(diagonal(), column, 0.0), axis=0, keepdims=True)


def to_column(row):
    return jnp.sum(jnp.where(diagonal(), row, 0.0), axis=1, keepdims=True)


def three_terms(x):
    high = x.astype(BF16).astype(F32)
    rest = x - high
    middle = rest.astype(BF16).astype(F32)
    return [high, middle, rest - middle]


def stat_rows(top, total):
    terms = three_terms(top) + three_terms(total)
    index = lax.broadcasted_iota(jnp.int32, (16, HEAD), 0)
    packed = jnp.zeros((16, HEAD), F32)
    for i, term in enumerate(terms):
        packed = jnp.where(index == i, term, packed)
    return packed.astype(BF16)


def read_stats(payload):
    stats = payload[PART_ROWS:PAY_ROWS].astype(F32)
    top = stats[0:1] + stats[1:2] + stats[2:3]
    total = stats[3:4] + stats[4:5] + stats[5:6]
    return top, total


def stack_queries(q, kh):
    heads = [q[:, h * HEAD : (h + 1) * HEAD].astype(F32) for h in range(kh * 8, kh * 8 + 8)]
    return jnp.concatenate(heads, axis=0).astype(BF16)


def partial_of(q, keys, values, allowed):
    x = jnp.where(allowed, nt_dot(q, keys), MASKED)
    top = jnp.max(x, axis=1, keepdims=True)
    weights = jnp.exp2((x - top) * SCALE2).astype(BF16)
    out = nn_dot(weights, jnp.concatenate([values, jnp.ones_like(values)], axis=1))
    return top, out[:, HEAD : HEAD + 1], out[:, :HEAD] / out[:, HEAD:]


def relative_group(step, other):
    group = lax.axis_index("req")
    chip = (lax.shift_right_logical(group, 1) - step) & 3
    return chip * 2 + ((group & 1) ^ other)


def passage_kernel(len_ref, req_ref, *refs):
    query_refs, (k_ref, v_ref), out_refs = refs[:4], refs[4:6], refs[6:]
    sender = my_sender()
    row_request = lax.shift_right_logical(lax.broadcasted_iota(jnp.int32, (64, 1), 0), 2) & 1
    lengths = [len_ref[j, sender] for j in range(PASSAGES)]
    requests = [req_ref[j, sender] for j in range(PASSAGES)]
    for index in range(GROUPS):
        step, other = index // 2, index % 2
        group = relative_group(step, other)
        begin, end, local, reach = jnp.int32(0), jnp.int32(0), jnp.int32(0), jnp.int32(0)
        for length, request in zip(lengths, requests):
            hit = lax.shift_right_logical(request, 1) == group
            begin = jnp.where(hit, reach, begin)
            reach = reach + length
            end = jnp.where(hit, reach, end)
            local = jnp.where(hit, request & 1, local)
        first = pl.multiple_of(jnp.minimum(begin & -TILE, ROWS - WINDOW), TILE)
        keys = first + lax.broadcasted_iota(jnp.int32, (64, WINDOW), 1)
        allowed = (keys >= begin) & (keys < end)
        q = query_refs[step][other]
        tops, totals = [], []
        for kh in range(2):
            lanes = slice(kh * HEAD, (kh + 1) * HEAD)
            top, total, out = partial_of(
                stack_queries(q, kh),
                k_ref[pl.ds(first, WINDOW), lanes],
                v_ref[pl.ds(first, WINDOW), lanes],
                allowed,
            )
            tops.append(jnp.where(row_request == local, top, MASKED))
            totals.append(total)
            out_refs[index][kh * 64 : (kh + 1) * 64] = out.astype(BF16)
        out_refs[index][PART_ROWS:PAY_ROWS] = stat_rows(
            to_row(jnp.concatenate(tops, axis=0)), to_row(jnp.concatenate(totals, axis=0))
        )


def passage_partials(queries, k, v, pass_len, pass_req):
    ins = [*queries, k, v]
    return pl.pallas_call(
        passage_kernel,
        grid_spec=pltpu.PrefetchScalarGridSpec(
            num_scalar_prefetch=2,
            grid=(1,),
            in_specs=[pl.BlockSpec(a.shape, lambda i, n, r, d=a.ndim: (0,) * d) for a in ins],
            out_specs=[pl.BlockSpec((PAY_ROWS, HEAD), lambda i, n, r: (0, 0))] * GROUPS,
        ),
        out_shape=[jax.ShapeDtypeStruct((PAY_ROWS, HEAD), BF16)] * GROUPS,
        compiler_params=pltpu.CompilerParams(vmem_limit_bytes=16 * 2**20),
        cost_estimate=pl.CostEstimate(flops=10**9, bytes_accessed=3 * 2**20, transcendentals=10**6),
        name="passage_partials",
    )(pass_len, pass_req, *ins)


def context_kernel(fill_ref, len_ref, req_ref, q_ref, ck_ref, cv_ref, dk_ref, dv_ref, out_ref, table_ref):
    fill_table(len_ref, req_ref, table_ref)
    row_request = lax.shift_right_logical(lax.broadcasted_iota(jnp.int32, (64, 1), 0), 2) & 1
    q = q_ref[...]
    context = ck_ref.shape[1]
    keys = lax.broadcasted_iota(jnp.int32, (64, context), 1)
    own_key = lax.broadcasted_iota(jnp.int32, (64, 8), 1)
    own_row = lax.broadcasted_iota(jnp.int32, (64, 8), 0) & 7
    same = lax.shift_right_logical(own_key, 2) == lax.shift_right_logical(own_row, 2)
    own_allowed = (own_key <= own_row) & same
    stats = [[], [], [], []]
    for kh in range(2):
        lanes = slice(kh * HEAD, (kh + 1) * HEAD)
        queries = stack_queries(q, kh)
        parts = [
            partial_of(queries, ck_ref[r, :, lanes], cv_ref[r, :, lanes], keys < fill_ref[0, r])
            for r in range(2)
        ]
        top, total, out = [jnp.where(row_request == 0, a, b) for a, b in zip(parts[0], parts[1])]
        out_ref[0, kh * 64 : (kh + 1) * 64] = out.astype(BF16)
        stats[0].append(top)
        stats[1].append(total)
        top, total, out = partial_of(queries, dk_ref[:, lanes], dv_ref[:, lanes], own_allowed)
        out_ref[1, kh * 64 : (kh + 1) * 64] = out.astype(BF16)
        stats[2].append(top)
        stats[3].append(total)
    rows = [to_row(jnp.concatenate(s, axis=0)) for s in stats]
    out_ref[0, PART_ROWS:PAY_ROWS] = stat_rows(rows[0], rows[1])
    out_ref[1, PART_ROWS:PAY_ROWS] = stat_rows(rows[2], rows[3])


def context_partials(q, ck, cv, dk, dv, pass_len, pass_req, fill):
    ins = [pass_len, pass_req, q, ck, cv, dk, dv]
    return pl.pallas_call(
        context_kernel,
        grid_spec=pltpu.PrefetchScalarGridSpec(
            num_scalar_prefetch=1,
            grid=(1,),
            in_specs=[pl.BlockSpec(a.shape, lambda i, f, d=a.ndim: (0,) * d) for a in ins],
            out_specs=[
                pl.BlockSpec((2, PAY_ROWS, HEAD), lambda i, f: (0, 0, 0)),
                pl.BlockSpec((8, 128), lambda i, f: (0, 0)),
            ],
        ),
        out_shape=[
            jax.ShapeDtypeStruct((2, PAY_ROWS, HEAD), BF16),
            jax.ShapeDtypeStruct((8, 128), jnp.int32),
        ],
        compiler_params=pltpu.CompilerParams(vmem_limit_bytes=16 * 2**20),
        cost_estimate=pl.CostEstimate(flops=10**9, bytes_accessed=3 * 2**20, transcendentals=10**6),
        name="context_partials",
    )(fill, *ins)


def combine(payloads):
    stats = [read_stats(p) for p in payloads]
    joint = functools.reduce(jnp.maximum, [top for top, _ in stats])
    shares = [total * jnp.exp2((top - joint) * SCALE2) for top, total in stats]
    total = functools.reduce(jnp.add, shares)
    out = jnp.zeros((PART_ROWS, HEAD), F32)
    for share, payload in zip(shares, payloads):
        out = out + to_column(share / total) * payload[:PART_ROWS].astype(F32)
    return joint, total, out


def merge_kernel(*refs):
    got_refs, own_ref, out_ref = refs[:GROUPS], refs[GROUPS], refs[GROUPS + 1]
    joint, total, out = combine([ref[...] for ref in got_refs] + [own_ref[0]])
    out_ref[:PART_ROWS] = out.astype(BF16)
    out_ref[PART_ROWS:PAY_ROWS] = stat_rows(joint, total)


def merge(got, own):
    return pl.pallas_call(
        merge_kernel,
        out_shape=jax.ShapeDtypeStruct((PAY_ROWS, HEAD), BF16),
        compiler_params=pltpu.CompilerParams(vmem_limit_bytes=8 * 2**20),
        name="merge_partials",
    )(*got, own)


def finish_kernel(*refs):
    got_refs, own_ref, out_ref = refs[:SHARDS], refs[SHARDS], refs[SHARDS + 1]
    _, _, out = combine([ref[...] for ref in got_refs] + [own_ref[1]])
    for h in range(16):
        out_ref[:, h * HEAD : (h + 1) * HEAD] = out[h * 8 : (h + 1) * 8].astype(BF16)


def finish(got, own):
    return pl.pallas_call(
        finish_kernel,
        out_shape=jax.ShapeDtypeStruct((8, 16 * HEAD), BF16),
        compiler_params=pltpu.CompilerParams(vmem_limit_bytes=8 * 2**20),
        name="finish_decode",
    )(*got, own)


def moved(x, axis, target):
    return lax.ppermute(x, axis, [(i, target(i)) for i in range(8)])


def shifted(x, d):
    return moved(x, "seq", lambda i: (i + d) % 8)


def group_step(i, step, other):
    return ((i // 2 + step) % 4) * 2 + (i % 2 ^ other)


def spread(pair, axis):
    return [pair] + [moved(pair, axis, lambda i, d=d: (i + d) % 8) for d in (2, 4, 6)]


def after(value, other):
    return lax.optimization_barrier((value, other))[0]


def body(
    q_pass,
    k_pass,
    passage_values,
    pass_len,
    pass_req,
    cache_fill,
    cache_k,
    cached_values,
    q_dec,
    decode_keys,
    decode_values,
):
    pass_len, pass_req, cache_fill = pass_len.T, pass_req.T, cache_fill.T
    peer = moved(q_dec, "req", lambda i: i ^ 1)
    send = after(pack(k_pass, passage_values, pass_len, pass_req), peer)
    got = lax.all_to_all(send, ("req", "seq"), split_axis=0, concat_axis=0, tiled=True)
    queries = spread(after(jnp.stack([q_dec, peer]), send), "req")
    half_out = passage_attention(
        q_pass, k_pass, passage_values, after(pass_len, queries[0]), 0, 5
    )
    to_groups = passage_partials(
        after(queries, half_out), k_pass, passage_values, pass_len, pass_req
    )
    from_groups = [to_groups[0]] + [
        moved(block, "req", lambda i, n=n: group_step(i, -(n // 2), n % 2))
        for n, block in enumerate(to_groups)
        if n > 0
    ]
    own, table = context_partials(
        q_dec,
        cache_k,
        cached_values,
        decode_keys,
        decode_values,
        pass_len,
        pass_req,
        after(cache_fill, to_groups),
    )
    pass_out = passage_attention(
        q_pass, k_pass, passage_values, after(pass_len, own), 5, 3, (half_out,)
    )
    part = merge(after(from_groups, pass_out), own)
    far = [shifted(part, d) for d in (5, 3, 4)]
    near = [shifted(part, d) for d in (1, 7)]
    parts = [part] + far + near + [shifted(x, d) for x, d in zip(near, (1, 7))]
    new_k, new_v = place(got, table)
    dec_out = finish(after(parts, new_k), own)
    return (pass_out, new_k, new_v, dec_out)


def solution(mesh):
    placed = (
        P(("req", "seq"), "tp"),
        P(("req", "seq"), "tp"),
        P(("req", "seq"), "tp"),
        P(),
        P(),
        P("req", "seq"),
        P("req", "seq", "tp"),
        P("req", "seq", "tp"),
        P("req", "tp"),
        P("req", "tp"),
        P("req", "tp"),
    )
    return jax.shard_map(
        body,
        mesh=mesh,
        in_specs=placed,
        out_specs=(
            P(("req", "seq"), "tp"),
            P("req", "seq", "tp"),
            P("req", "seq", "tp"),
            P("req", "tp"),
        ),
        check_vma=False,
    )
```
